128 devices in a mesh: layer: 8 (over x_lo, y), plane: 16 (over z, x_hi, core).
Axes of the slice: x: 4 (x_hi: 2, x_lo: 2; x = x_hi * 2 + x_lo), y: 4, z: 4, core: 2. Of those that a mesh axis runs over, the one named last changes fastest.
Arguments:
- rhs: float32 [2, 8, 768, 32, 128], P(None, None, 'layer', 'plane'), may hold values from -6 to 6
- inverse_blocks: bfloat16 [8, 2, 32, 128, 2, 32, 128], P('layer', None, 'plane')
- mode_panel: bfloat16 [256, 32, 128], P(None, 'plane'), may hold values from -5 to 5
- mode_profile: bfloat16 [256, 768], P('plane', 'layer'), may hold values from -5 to 5
- generator: int32 [256], replicated, may hold values from 1 to 32767
- lattice_index: int32 [8], replicated, may hold values from 0 to 32767
- shift_index: int32 [8, 256], replicated, may hold values from 0 to 32767
Outputs:
- solution: float32 [2, 8, 768, 32, 128], P(None, None, 'layer', 'plane')
- residual: float32 [2, 8, 768, 32, 128], P(None, None, 'layer', 'plane')
The draws below stay inside these ranges and needn't reach their ends.
All inputs are finite; a program needn't handle non-finite values.
Results may differ from the reference program's by a relative error of at most 0.0033.
Values may be sent and summed in bfloat16 or wider, within the bound.
No kernel may reach another device: no remote copies, remote signals or barrier semaphores. Data moves between devices by JAX's collectives and lax.ppermute only.
A program may use at most 128 MiB of HBM per device.

```python
import jax
import jax.numpy as jnp
from jax import lax

NY = 128
LZ = 96
R = 8
MODES = 256
NPTS = 32768
NX = 32
GROUPS = 8
NZ = 768


def draw_inverse_blocks(key, part):
    key = jax.random.fold_in(key, 7)
    shape = (GROUPS, 2, NX, NY, 2, NX, NY)
    noise_key, diag_key = jax.random.split(key)
    spread = 0.5 / jnp.sqrt(jnp.float32(2 * NX * NY))
    noise = jax.random.normal(noise_key, shape, jnp.float32)
    diagonal = 0.8 + 0.4 * jax.random.uniform(diag_key, shape, jnp.float32)
    same = lax.broadcasted_iota(jnp.int32, shape, 1) == lax.broadcasted_iota(jnp.int32, shape, 4)
    same = same & (lax.broadcasted_iota(jnp.int32, shape, 2) == lax.broadcasted_iota(jnp.int32, shape, 5))
    same = same & (lax.broadcasted_iota(jnp.int32, shape, 3) == lax.broadcasted_iota(jnp.int32, shape, 6))
    values = spread * noise + jnp.where(same, diagonal, 0.0)
    return values.astype(jnp.bfloat16)


def with_ends(values, rng, smallest, largest):
    longest = values.shape.index(max(values.shape))
    spots = []
    for shift in (0, 1):
        where = [jax.random.randint(jax.random.fold_in(rng, axis), (), 0, length) for axis, length in enumerate(values.shape)]
        where[longest] = (where[longest] + shift) % values.shape[longest]
        spots.append(tuple(where))
    return values.at[spots[0]].set(smallest).at[spots[1]].set(largest)


def block_scale(rng, extent, cuts, least, largest):
    loudness, own = 1.0, jax.random.fold_in(rng, 6)
    for dim, blocks in cuts:
        heights = jnp.exp(jax.random.uniform(jax.random.fold_in(own, dim), (blocks,), jnp.float32, least / len(cuts), largest / len(cuts)))
        loudness = loudness * jnp.repeat(heights, extent[dim] // blocks).reshape([-1 if axis == dim else 1 for axis in range(len(extent))])
    return loudness


def scatter_about(rng, shape, width, limit, shards=(), kind=jnp.bfloat16):
    drawn = width * jax.random.normal(rng, shape, jnp.float32)
    if shards:
        drawn = drawn * block_scale(rng, shape, shards, -0.22, 0.18)
    return jnp.clip(drawn, -limit, limit).astype(kind)


def setup_inputs(seed: int = 0) -> dict:
    seeds = jax.random.split(jax.random.key(seed), 8)
    rhs = scatter_about(seeds[0], (2, R, NZ, NX, NY), 1.0, 6.0, ((2, 8), (3, 16)), jnp.float32)
    inverse_blocks = draw_inverse_blocks(jax.random.fold_in(seeds[7], 71), 0)
    mode_panel = scatter_about(seeds[2], (MODES, NX, NY), 1.0, 5.0, ((1, 16),))
    mode_profile = scatter_about(seeds[3], (MODES, NZ), 1.0, 5.0, ((0, 16), (1, 8)))
    generator = with_ends(jax.random.randint(seeds[4], (MODES,), 1, NPTS), jax.random.fold_in(seeds[4], 1), 1, NPTS - 1).astype(jnp.int32)
    lattice_index = with_ends(jax.random.randint(seeds[5], (R,), 0, NPTS), jax.random.fold_in(seeds[5], 1), 0, NPTS - 1).astype(jnp.int32)
    shift_index = with_ends(jax.random.randint(seeds[6], (R, MODES), 0, NPTS), jax.random.fold_in(seeds[6], 1), 0, NPTS - 1).astype(jnp.int32)
    return dict(rhs=rhs, inverse_blocks=inverse_blocks, mode_panel=mode_panel, mode_profile=mode_profile, generator=generator, lattice_index=lattice_index, shift_index=shift_index)


COUPLING = 0.8
ABSORB_RATE = 0.3
WAVE_SCALE = 0.8

def as_columns(block_rhs):
    layers = block_rhs.shape[2]
    return block_rhs.transpose(0, 3, 4, 1, 2).reshape(2 * NX * NY, R * layers)

def from_columns(matrix, layers):
    return matrix.reshape(2, NX, NY, R, layers).transpose(0, 3, 4, 1, 2)

def reference(rhs, inverse_blocks, mode_panel, mode_profile, generator, lattice_index, shift_index):
    rounded = rhs.astype(jnp.bfloat16)
    pieces = []
    interface = None
    for group in range(GROUPS):
        matrix = inverse_blocks[group].reshape(2 * NX * NY, 2 * NX * NY)
        part_rhs = rounded[:, :, group * LZ:(group + 1) * LZ]
        fronts = from_columns(jnp.dot(matrix, as_columns(part_rhs), preferred_element_type=jnp.float32), LZ)
        first = fronts[:, :, 0:1]
        if group > 0:
            coupled = jnp.dot(matrix, as_columns(interface.astype(jnp.bfloat16)), preferred_element_type=jnp.float32)
            first = first + COUPLING * from_columns(coupled, 1)
        interface = first
        pieces.append(jnp.concatenate([first, fronts[:, :, 1:]], axis=2))
    solution = jnp.concatenate(pieces, axis=2)
    mixed = (lattice_index[:, None] * generator[None, :] + shift_index) % NPTS
    amplitude = 0.25 / jnp.sqrt(1.0 + jnp.arange(MODES, dtype=jnp.float32) / 8.0)
    coef = amplitude[None, :] * ((mixed.astype(jnp.float32) + 0.5) / NPTS - 0.5)
    weights = coef[:, :, None] * mode_profile.astype(jnp.float32)[None, :, :]
    logc = jnp.einsum('rkz,kxy->rzxy', weights, mode_panel.astype(jnp.float32), precision=lax.Precision.HIGHEST)
    wavenum = WAVE_SCALE * jnp.exp(-2.0 * logc)
    padded = jnp.pad(solution, ((0, 0), (0, 0), (1, 1), (1, 1), (1, 1)))
    beside = padded[:, :, 2:, 1:-1, 1:-1] + padded[:, :, :-2, 1:-1, 1:-1]
    beside = beside + padded[:, :, 1:-1, 2:, 1:-1] + padded[:, :, 1:-1, :-2, 1:-1]
    beside = beside + padded[:, :, 1:-1, 1:-1, 2:] + padded[:, :, 1:-1, 1:-1, :-2]
    lap = 6.0 * solution - beside
    real_part = solution[0]
    imag_part = solution[1]
    apply_real = lap[0] - wavenum * real_part + ABSORB_RATE * wavenum * imag_part
    apply_imag = lap[1] - wavenum * imag_part - ABSORB_RATE * wavenum * real_part
    residual = rhs - jnp.stack([apply_real, apply_imag])
    return (solution, residual)
```

```python
import jax
import jax.numpy as jnp
from jax import lax
from jax.experimental import pallas as pl
from jax.experimental.pallas import tpu as pltpu
from jax.sharding import PartitionSpec as P

MODES = 256
NPTS = 32768
COUPLING = 0.8
ABSORB_RATE = 0.3
WAVE_SCALE = 0.8

G = 8
D = 16
LZ = 96
R = 8
K = 512
NY = 128

bf16 = jnp.bfloat16
f32 = jnp.float32
VMEM = pltpu.VMEM


def whole(space=VMEM):
    return pl.BlockSpec(memory_space=space)


def params(mib):
    return pltpu.CompilerParams(vmem_limit_bytes=mib * 2**20)


def dot_t(x, h):
    return lax.dot_general(x, h, (((1,), (1,)), ((), ())), preferred_element_type=f32)


def prepare_kernel(rhs_ref, profile_ref, x_ref, chunk_ref):
    chunk_ref[0] = jnp.zeros((32, K), bf16)
    for a in range(2):
        for x in range(2):
            cols = pl.ds(a * 256 + x * NY, NY)
            for r in range(R):
                x_ref[pl.ds(r * LZ, LZ), cols] = rhs_ref[a, r, pl.ds(x, LZ, stride=2), :].astype(bf16)
    head = jnp.concatenate([rhs_ref[a, :, x, :] for a in range(2) for x in range(2)], axis=1)
    profile = jnp.concatenate([profile_ref[...], jnp.zeros((16, K - LZ), bf16)], axis=1)
    chunk = jnp.concatenate([head, jnp.zeros((8, K), f32)], axis=0).astype(bf16)
    for i in range(D):
        chunk_ref[i, pl.ds(0, 16), :] = chunk
        chunk_ref[i, pl.ds(16, 16), :] = profile


def prepare(rhs, profile):
    return pl.pallas_call(
        prepare_kernel,
        out_shape=(jax.ShapeDtypeStruct((R * LZ, K), bf16), jax.ShapeDtypeStruct((D, 32, K), bf16)),
        in_specs=[whole(), whole()],
        out_specs=(whole(), whole()),
        compiler_params=params(8),
    )(rhs, profile)


def arrange_kernel(blocks_ref, out_ref):
    m = lax.broadcasted_iota(jnp.int32, (256, 256), 0)
    n = lax.broadcasted_iota(jnp.int32, (256, 256), 1)
    swap = ((m // 16 == n % 16) & (m % 16 == n // 16)).astype(f32).astype(bf16)

    def body(b_ref):
        base = pl.multiple_of(pl.program_id(0) * 32, 32)
        for s in range(2):
            for c in range(2):
                for half in range(2):
                    tile = b_ref[pl.ds(s * 16, 16), c, pl.ds(half * 16, 16), :].reshape(256, NY)
                    moved = jnp.dot(swap, tile, preferred_element_type=f32).astype(bf16)
                    for q in range(16):
                        p = half * 16 + q
                        out_ref[p // 2, pl.ds(base + s * 16, 16), pl.ds(c * 256 + (p % 2) * NY, NY)] = moved[
                            q * 16 : (q + 1) * 16
                        ]

    pltpu.emit_pipeline(
        body, grid=(K // 32,), in_specs=[pl.BlockSpec((32, 2, 32, NY), lambda i: (i, 0, 0, 0))]
    )(blocks_ref)


def arrange(blocks):
    return pl.pallas_call(
        arrange_kernel,
        out_shape=jax.ShapeDtypeStruct((D, K, K), bf16),
        in_specs=[whole(pl.ANY)],
        out_specs=whole(),
        compiler_params=params(14),
        cost_estimate=pl.CostEstimate(flops=2 * 10**9, bytes_accessed=17 * 10**6, transcendentals=0),
    )(blocks)


def first_kernel(h_ref, x_ref, v_ref, out_ref):
    acc = jnp.zeros((16, K), f32)
    for i in range(D):
        acc = acc + dot_t(x_ref[i, pl.ds(0, 16), :], h_ref[i])
    v = acc[:R]
    v_ref[...] = v
    for i in range(2 * D):
        out_ref[i] = v.astype(bf16)


def step_kernel(mine_ref, h_ref, x_ref, base_ref, old_ref, v_ref, out_ref):
    acc = jnp.zeros((R, K), f32)
    for i in range(D):
        acc = acc + dot_t(x_ref[i], h_ref[i])
    v = jnp.where(mine_ref[0] > 0, base_ref[...] + COUPLING * acc, old_ref[...])
    v_ref[...] = v
    for i in range(2 * D):
        out_ref[i] = v.astype(bf16)


MATVEC_OUT = (jax.ShapeDtypeStruct((R, K), f32), jax.ShapeDtypeStruct((2 * D, R, K), bf16))
MATVEC_COST = pl.CostEstimate(flops=10**8, bytes_accessed=8 * 10**6, transcendentals=0)


def first_product(h, x):
    return pl.pallas_call(
        first_kernel,
        out_shape=MATVEC_OUT,
        in_specs=[whole()] * 2,
        out_specs=(whole(), whole()),
        compiler_params=params(12),
        cost_estimate=MATVEC_COST,
    )(h, x)


def step_product(mine, h, x, base, old):
    return pl.pallas_call(
        step_kernel,
        out_shape=MATVEC_OUT,
        in_specs=[whole(pltpu.SMEM)] + [whole()] * 4,
        out_specs=(whole(), whole()),
        compiler_params=params(12),
        cost_estimate=MATVEC_COST,
    )(mine, h, x, base, old)


def fronts_kernel(x_ref, h_ref, y_ref, low_ref, high_ref, last_ref):
    acc = jnp.zeros((2 * LZ, K), f32)
    for i in range(D):
        acc = acc + dot_t(x_ref[i], h_ref[i])
    acc = acc.reshape(2, LZ, K)
    y_ref[...] = acc
    for r in range(2):
        for a in range(2):
            low_ref[r, a] = acc[r, :, a * 256 : a * 256 + NY].astype(bf16)
            high_ref[r, a] = acc[r, :, a * 256 + NY : a * 256 + 256].astype(bf16)
        last_ref[r] = acc[r, LZ - 16 :, :].astype(bf16)


def fronts_of(x, h, part):
    return pl.pallas_call(
        fronts_kernel,
        grid=(2,),
        out_shape=(
            jax.ShapeDtypeStruct((4, LZ, K), f32),
            jax.ShapeDtypeStruct((4, 2, LZ, NY), bf16),
            jax.ShapeDtypeStruct((4, 2, LZ, NY), bf16),
            jax.ShapeDtypeStruct((4, 16, K), bf16),
        ),
        in_specs=[pl.BlockSpec((D, 2 * LZ, K), lambda i: (0, 2 * part + i, 0)), whole()],
        out_specs=(
            pl.BlockSpec((2, LZ, K), lambda i: (i, 0, 0)),
            pl.BlockSpec((2, 2, LZ, NY), lambda i: (i, 0, 0, 0)),
            pl.BlockSpec((2, 2, LZ, NY), lambda i: (i, 0, 0, 0)),
            pl.BlockSpec((2, 16, K), lambda i: (i, 0, 0)),
        ),
        compiler_params=params(18),
        cost_estimate=pl.CostEstimate(flops=3 * 10**9, bytes_accessed=15 * 10**6, transcendentals=0),
    )(x, h)


def wave_kernel(x_ref, coef_ref, panel_ref, out_ref):
    profile = jnp.concatenate([x_ref[i, pl.ds(16, 16), :][:, :LZ] for i in range(D)], axis=0).astype(f32)
    panel = panel_ref[...]
    for r in range(R):
        weights = profile * coef_ref[:, r : r + 1]
        log = jnp.zeros((LZ, 256), f32)
        for _ in range(3):
            term = weights.astype(bf16)
            weights = weights - term.astype(f32)
            log = log + lax.dot_general(term, panel, (((0,), (0,)), ((), ())), preferred_element_type=f32)
        out_ref[r] = WAVE_SCALE * jnp.exp(-2.0 * log)


def wave(x, coef, panel):
    return pl.pallas_call(
        wave_kernel,
        out_shape=jax.ShapeDtypeStruct((R, LZ, 256), f32),
        in_specs=[whole()] * 3,
        out_specs=whole(),
        compiler_params=params(8),
        cost_estimate=pl.CostEstimate(flops=3 * 10**8, bytes_accessed=2 * 10**6, transcendentals=2 * 10**5),
    )(x, coef, panel)


def residual_kernel(ya, yb, rhs_ref, la, lb, ha, hb, pa, pb, v_ref, nl_ref, vl_ref, vh_ref, wave_ref, sol_ref, res_ref):
    row = lax.broadcasted_iota(jnp.int32, (LZ, NY), 0)
    lane = lax.broadcasted_iota(jnp.int32, (LZ, NY), 1)
    for r in range(R):
        y_ref, low_ref, high_ref, prev_ref = (ya, la, ha, pa) if r < 4 else (yb, lb, hb, pb)
        k = r % 4
        s = {}
        for a in range(2):
            for x in range(2):
                cols = slice(a * 256 + x * NY, a * 256 + (x + 1) * NY)
                s[a, x] = jnp.where(row == 0, v_ref[r : r + 1, cols], y_ref[k, :, cols])
        lap = {}
        for a in range(2):
            below = jnp.where(row == 0, vl_ref[r : r + 1, a * NY : (a + 1) * NY].astype(f32), low_ref[k, a].astype(f32))
            above = jnp.where(row == 0, vh_ref[r : r + 1, a * NY : (a + 1) * NY].astype(f32), high_ref[k, a].astype(f32))
            for x in range(2):
                cols = slice(a * 256 + x * NY, a * 256 + (x + 1) * NY)
                own = s[a, x]
                before = jnp.where(row == 0, prev_ref[k, :, cols][15:16].astype(f32), pltpu.roll(own, 1, 0))
                after = jnp.where(row == LZ - 1, nl_ref[r : r + 1, cols].astype(f32), pltpu.roll(own, LZ - 1, 0))
                left = jnp.where(lane == 0, 0.0, pltpu.roll(own, 1, 1))
                right = jnp.where(lane == NY - 1, 0.0, pltpu.roll(own, NY - 1, 1))
                beside = before + after + left + right
                beside = beside + (below if x == 0 else s[a, 0]) + (s[a, 1] if x == 0 else above)
                lap[a, x] = 6.0 * own - beside
        for x in range(2):
            w = wave_ref[r, :, x * NY : (x + 1) * NY]
            rows = pl.ds(x, LZ, stride=2)
            real = lap[0, x] - w * s[0, x] + ABSORB_RATE * w * s[1, x]
            imag = lap[1, x] - w * s[1, x] - ABSORB_RATE * w * s[0, x]
            sol_ref[0, r, rows, :] = s[0, x]
            sol_ref[1, r, rows, :] = s[1, x]
            res_ref[0, r, rows, :] = rhs_ref[0, r, rows, :] - real
            res_ref[1, r, rows, :] = rhs_ref[1, r, rows, :] - imag


def residual(*args):
    shape = jax.ShapeDtypeStruct((2, R, 2 * LZ, NY), f32)
    return pl.pallas_call(
        residual_kernel,
        out_shape=(shape, shape),
        in_specs=[whole()] * len(args),
        out_specs=(whole(), whole()),
        compiler_params=params(24),
    )(*args)


def pair_groups(step):
    groups = []
    for k in range(G // 2):
        first = (2 * k + step - 1) % G
        second = (first + 1) % G
        groups.append([first * D + i for i in range(D)] + [second * D + i for i in range(D)])
    return groups


def shift(value, axis, by):
    size = lax.axis_size(axis)
    return lax.ppermute(value, axis, [(i, i + by) for i in range(size) if 0 <= i + by < size])


def shards(rhs, inverse_blocks, mode_panel, mode_profile, generator, lattice_index, shift_index):
    group = lax.axis_index("layer")
    flat = rhs.reshape(2, R, 2 * LZ, NY)
    own, chunk = prepare(flat, mode_profile)
    gathered = lax.all_gather(own, "plane", axis=0)
    heads = lax.all_to_all(chunk, "plane", 0, 0)
    h = arrange(inverse_blocks.reshape(K, 2, 32, NY))

    mixed = (lattice_index[None, :] * generator[:, None] + shift_index.T) % NPTS
    amplitude = 0.25 / jnp.sqrt(1.0 + jnp.arange(MODES, dtype=f32) / 8.0)
    coef = amplitude[:, None] * ((mixed.astype(f32) + 0.5) / NPTS - 0.5)
    wavenum = wave(heads, coef, mode_panel.reshape(MODES, 256))

    base, out = first_product(h, heads)
    v = base
    for step in range(1, G):
        got = lax.all_to_all(out, ("layer", "plane"), 0, 0, axis_index_groups=pair_groups(step))
        mine = (group == step).astype(jnp.int32).reshape(1)
        v, out = step_product(mine, h, got, base, v)

    ya, sla, sha, ta = fronts_of(gathered, h, 0)
    yb, slb, shb, tb = fronts_of(gathered, h, 1)
    la, lb = shift(sha, "plane", 1), shift(shb, "plane", 1)
    ha, hb = shift(sla, "plane", -1), shift(slb, "plane", -1)
    pa, pb = shift(ta, "layer", 1), shift(tb, "layer", 1)
    vb = v.astype(bf16)
    nl = shift(vb, "layer", -1)
    vl = shift(jnp.concatenate([vb[:, NY : 2 * NY], vb[:, 3 * NY :]], axis=1), "plane", 1)
    vh = shift(jnp.concatenate([vb[:, :NY], vb[:, 2 * NY : 3 * NY]], axis=1), "plane", -1)
    sol, res = residual(ya, yb, flat, la, lb, ha, hb, pa, pb, v, nl, vl, vh, wavenum)
    return sol.reshape(rhs.shape), res.reshape(rhs.shape)


def solution(mesh):
    return jax.shard_map(
        shards,
        mesh=mesh,
        in_specs=(
            P(None, None, "layer", "plane", None),
            P("layer", None, "plane", None, None, None, None),
            P(None, "plane", None),
            P("plane", "layer"),
            P(),
            P(),
            P(),
        ),
        out_specs=(P(None, None, "layer", "plane", None), P(None, None, "layer", "plane", None)),
        check_vma=False,
    )
```

```python
import jax
import jax.numpy as jnp
from jax import lax
from jax.experimental import pallas as pl
from jax.experimental.pallas import tpu as pltpu
from jax.sharding import PartitionSpec as P

MODES = 256
NPTS = 32768
COUPLING = 0.8
ABSORB_RATE = 0.3
WAVE_SCALE = 0.8

G = 8
D = 16
C = 8
LZ = 96
R = 8
K = 512
NY = 128

bf16 = jnp.bfloat16
f32 = jnp.float32
VMEM = pltpu.VMEM


def whole(space=VMEM):
    return pl.BlockSpec(memory_space=space)


def params(mib):
    return pltpu.CompilerParams(vmem_limit_bytes=mib * 2**20)


def dot_t(x, h):
    return lax.dot_general(x, h, (((1,), (1,)), ((), ())), preferred_element_type=f32)


def prepare_kernel(rhs_ref, profile_ref, x_ref, chunk_ref):
    chunk_ref[0] = jnp.zeros((32, K), bf16)
    for a in range(2):
        for x in range(2):
            cols = pl.ds(a * 256 + x * NY, NY)
            for r in range(R):
                x_ref[pl.ds(r * LZ, LZ), cols] = rhs_ref[a, r, pl.ds(x, LZ, stride=2), :].astype(bf16)
    head = jnp.concatenate([rhs_ref[a, :, x, :] for a in range(2) for x in range(2)], axis=1)
    profile = jnp.concatenate([profile_ref[...], jnp.zeros((16, K - LZ), bf16)], axis=1)
    chunk = jnp.concatenate([head, jnp.zeros((8, K), f32)], axis=0).astype(bf16)
    for i in range(D):
        chunk_ref[i, pl.ds(0, 16), :] = chunk
        chunk_ref[i, pl.ds(16, 16), :] = profile


def prepare(rhs, profile):
    return pl.pallas_call(
        prepare_kernel,
        out_shape=(jax.ShapeDtypeStruct((R * LZ, K), bf16), jax.ShapeDtypeStruct((D, 32, K), bf16)),
        in_specs=[whole(), whole()],
        out_specs=(whole(), whole()),
        compiler_params=params(8),
    )(rhs, profile)


def arrange_kernel(blocks_ref, h_ref):
    m = lax.broadcasted_iota(jnp.int32, (256, 256), 0)
    n = lax.broadcasted_iota(jnp.int32, (256, 256), 1)
    swap = ((m // 16 == n % 16) & (m % 16 == n // 16)).astype(f32).astype(bf16)

    def body(b_ref, out_ref):
        for s in range(2):
            for c in range(2):
                for half in range(2):
                    tile = b_ref[pl.ds(s * 16, 16), c, pl.ds(half * 16, 16), :].reshape(256, NY)
                    moved = jnp.dot(swap, tile, preferred_element_type=f32).astype(bf16)
                    for q in range(16):
                        p = half * 16 + q
                        source = p // 2
                        out_ref[source % 2, source // 2, pl.ds(s * 16, 16), pl.ds(c * 256 + (p % 2) * NY, NY)] = moved[
                            q * 16 : (q + 1) * 16
                        ]

    pltpu.emit_pipeline(
        body,
        grid=(K // 32,),
        in_specs=[pl.BlockSpec((32, 2, 32, NY), lambda i: (i, 0, 0, 0))],
        out_specs=[pl.BlockSpec((2, C, 32, K), lambda i: (0, 0, i, 0))],
    )(blocks_ref, h_ref)


def arrange(blocks):
    return pl.pallas_call(
        arrange_kernel,
        out_shape=jax.ShapeDtypeStruct((2, C, K, K), bf16),
        in_specs=[whole(pltpu.HBM)],
        out_specs=whole(pltpu.HBM),
        compiler_params=params(50),
        cost_estimate=pl.CostEstimate(flops=2 * 10**9, bytes_accessed=17 * 10**6, transcendentals=0),
    )(blocks)


COST = pl.CostEstimate(flops=10**8, bytes_accessed=5 * 10**6, transcendentals=0)
CHUNK = 2


def stream(h_ref, acc_ref, core, operand):
    def body(b_ref):
        first = pl.program_id(0) * CHUNK
        for j in range(CHUNK):
            acc_ref[...] += dot_t(operand(first + j), b_ref[j])

    pltpu.emit_pipeline(
        body, grid=(C // CHUNK,), in_specs=[pl.BlockSpec((None, CHUNK, K, K), lambda k: (core, k, 0, 0))]
    )(h_ref)


def first_kernel(h_ref, x_ref, v_ref, out_ref, acc_ref):
    acc_ref[...] = jnp.zeros((16, K), f32)
    for core in range(2):
        stream(h_ref, acc_ref, core, lambda k: x_ref[2 * k + core, pl.ds(0, 16), :])
    v = acc_ref[pl.ds(0, R), :]
    v_ref[...] = v
    for i in range(D):
        out_ref[i] = v.astype(bf16)


def first_product(h, x):
    return pl.pallas_call(
        first_kernel,
        out_shape=MATVEC_OUT,
        in_specs=[whole(pltpu.HBM), whole()],
        out_specs=(whole(), whole()),
        scratch_shapes=[VMEM((16, K), f32)],
        compiler_params=params(50),
        cost_estimate=COST,
    )(h, x)


def own_kernel(core_ref, h_ref, x_ref, behind_ref, acc_ref):
    acc_ref[...] = jnp.zeros((R, K), f32)
    stream(h_ref, acc_ref, core_ref[0], lambda k: x_ref[k])


def own_half(core, h, x, behind):
    return pl.pallas_call(
        own_kernel,
        out_shape=jax.ShapeDtypeStruct((R, K), f32),
        in_specs=[whole(pltpu.SMEM), whole(pltpu.HBM), whole(), whole(pl.ANY)],
        out_specs=whole(),
        compiler_params=params(50),
        cost_estimate=COST,
    )(core, h, x, behind)


def other_kernel(core_ref, mine_ref, h_ref, x_ref, half_ref, base_ref, old_ref, v_ref, out_ref, acc_ref):
    acc_ref[...] = half_ref[...]
    stream(h_ref, acc_ref, 1 - core_ref[0], lambda k: x_ref[k])
    v = jnp.where(mine_ref[0] > 0, base_ref[...] + COUPLING * acc_ref[...], old_ref[...])
    v_ref[...] = v
    for i in range(D):
        out_ref[i] = v.astype(bf16)


MATVEC_OUT = (jax.ShapeDtypeStruct((R, K), f32), jax.ShapeDtypeStruct((D, R, K), bf16))


def other_half(core, mine, h, x, half, base, old):
    return pl.pallas_call(
        other_kernel,
        out_shape=MATVEC_OUT,
        in_specs=[whole(pltpu.SMEM)] * 2 + [whole(pltpu.HBM)] + [whole()] * 4,
        out_specs=(whole(), whole()),
        scratch_shapes=[VMEM((R, K), f32)],
        compiler_params=params(50),
        cost_estimate=COST,
    )(core, mine, h, x, half, base, old)


def fronts_kernel(x_ref, h_ref, behind_ref, y_ref, low_ref, high_ref, last_ref):
    def body(x_block, h_block):
        @pl.when(pl.program_id(0) == 0)
        def _():
            y_ref[...] = jnp.zeros((R, LZ, K), f32)

        for part in range(4):
            rows = pl.ds(part * 2 * LZ, 2 * LZ)
            y_ref[pl.ds(2 * part, 2)] += dot_t(x_block[rows, :], h_block[...]).reshape(2, LZ, K)

    pltpu.emit_pipeline(
        body,
        grid=(D,),
        in_specs=[
            pl.BlockSpec((None, R * LZ, K), lambda i: (i, 0, 0)),
            pl.BlockSpec((None, None, K, K), lambda i: (lax.rem(i, 2), lax.div(i, 2), 0, 0)),
        ],
    )(x_ref, h_ref)
    for r in range(R):
        for a in range(2):
            low_ref[r, a] = y_ref[r, :, a * 256 : a * 256 + NY].astype(bf16)
            high_ref[r, a] = y_ref[r, :, a * 256 + NY : a * 256 + 256].astype(bf16)
    last_ref[...] = jnp.concatenate([y_ref[r, LZ - 1 : LZ, :] for r in range(R)], axis=0).astype(bf16)


def fronts_of(x, h, behind):
    halo = jax.ShapeDtypeStruct((R, 2, LZ, NY), bf16)
    return pl.pallas_call(
        fronts_kernel,
        out_shape=(jax.ShapeDtypeStruct((R, LZ, K), f32), halo, halo, jax.ShapeDtypeStruct((R, K), bf16)),
        in_specs=[whole(pltpu.HBM), whole(pltpu.HBM), whole(pl.ANY)],
        out_specs=(whole(),) * 4,
        compiler_params=params(50),
        cost_estimate=pl.CostEstimate(flops=6 * 10**9, bytes_accessed=23 * 10**6, transcendentals=0),
    )(x, h, behind)


def wave_kernel(x_ref, coef_ref, panel_ref, behind_ref, out_ref):
    profile = jnp.concatenate([x_ref[i, pl.ds(16, 16), :][:, :LZ] for i in range(D)], axis=0).astype(f32)
    panel = panel_ref[...]
    for r in range(R):
        weights = profile * coef_ref[:, r : r + 1]
        log = jnp.zeros((LZ, 256), f32)
        for _ in range(3):
            term = weights.astype(bf16)
            weights = weights - term.astype(f32)
            log = log + lax.dot_general(term, panel, (((0,), (0,)), ((), ())), preferred_element_type=f32)
        out_ref[r] = WAVE_SCALE * jnp.exp(-2.0 * log)


def wave(x, coef, panel, behind):
    return pl.pallas_call(
        wave_kernel,
        out_shape=jax.ShapeDtypeStruct((R, LZ, 256), f32),
        in_specs=[whole()] * 3 + [whole(pl.ANY)],
        out_specs=whole(),
        compiler_params=params(8),
        cost_estimate=pl.CostEstimate(flops=3 * 10**8, bytes_accessed=2 * 10**6, transcendentals=2 * 10**5),
    )(x, coef, panel, behind)


def residual_kernel(y_ref, rhs_ref, low_ref, high_ref, prev_ref, v_ref, nl_ref, vl_ref, vh_ref, wave_ref, sol_ref, res_ref):
    row = lax.broadcasted_iota(jnp.int32, (LZ, NY), 0)
    lane = lax.broadcasted_iota(jnp.int32, (LZ, NY), 1)
    for r in range(R):
        s = {}
        for a in range(2):
            for x in range(2):
                cols = slice(a * 256 + x * NY, a * 256 + (x + 1) * NY)
                s[a, x] = jnp.where(row == 0, v_ref[r : r + 1, cols], y_ref[r, :, cols])
        lap = {}
        for a in range(2):
            below = jnp.where(row == 0, vl_ref[r : r + 1, a * NY : (a + 1) * NY].astype(f32), low_ref[r, a].astype(f32))
            above = jnp.where(row == 0, vh_ref[r : r + 1, a * NY : (a + 1) * NY].astype(f32), high_ref[r, a].astype(f32))
            for x in range(2):
                cols = slice(a * 256 + x * NY, a * 256 + (x + 1) * NY)
                own = s[a, x]
                before = jnp.where(row == 0, prev_ref[r : r + 1, cols].astype(f32), pltpu.roll(own, 1, 0))
                after = jnp.where(row == LZ - 1, nl_ref[r : r + 1, cols].astype(f32), pltpu.roll(own, LZ - 1, 0))
                left = jnp.where(lane == 0, 0.0, pltpu.roll(own, 1, 1))
                right = jnp.where(lane == NY - 1, 0.0, pltpu.roll(own, NY - 1, 1))
                beside = before + after + left + right
                beside = beside + (below if x == 0 else s[a, 0]) + (s[a, 1] if x == 0 else above)
                lap[a, x] = 6.0 * own - beside
        for x in range(2):
            w = wave_ref[r, :, x * NY : (x + 1) * NY]
            rows = pl.ds(x, LZ, stride=2)
            real = lap[0, x] - w * s[0, x] + ABSORB_RATE * w * s[1, x]
            imag = lap[1, x] - w * s[1, x] - ABSORB_RATE * w * s[0, x]
            sol_ref[0, r, rows, :] = s[0, x]
            sol_ref[1, r, rows, :] = s[1, x]
            res_ref[0, r, rows, :] = rhs_ref[0, r, rows, :] - real
            res_ref[1, r, rows, :] = rhs_ref[1, r, rows, :] - imag


def residual(*args):
    shape = jax.ShapeDtypeStruct((2, R, 2 * LZ, NY), f32)
    return pl.pallas_call(
        residual_kernel,
        out_shape=(shape, shape),
        in_specs=[whole()] * len(args),
        out_specs=(whole(), whole()),
        compiler_params=params(24),
    )(*args)


def pair_groups(step):
    groups = []
    for k in range(G // 2):
        first = (2 * k + step - 1) % G
        second = (first + 1) % G
        for core in range(2):
            groups.append([g * D + 2 * i + core for g in (first, second) for i in range(C)])
    return groups


def shift(value, axis, by):
    size = lax.axis_size(axis)
    return lax.ppermute(value, axis, [(i, i + by) for i in range(size) if 0 <= i + by < size])


def shards(rhs, inverse_blocks, mode_panel, mode_profile, generator, lattice_index, shift_index):
    group = lax.axis_index("layer")
    flat = rhs.reshape(2, R, 2 * LZ, NY)
    own, chunk = prepare(flat, mode_profile)
    gathered = lax.all_gather(own, "plane", axis=0)
    heads = lax.all_to_all(chunk, "plane", 0, 0)
    h = arrange(inverse_blocks.reshape(K, 2, 32, NY))

    mixed = (lattice_index[None, :] * generator[:, None] + shift_index.T) % NPTS
    amplitude = 0.25 / jnp.sqrt(1.0 + jnp.arange(MODES, dtype=f32) / 8.0)
    coef = amplitude[:, None] * ((mixed.astype(f32) + 0.5) / NPTS - 0.5)
    core = lax.rem(lax.axis_index("plane"), 2).astype(jnp.int32).reshape(1)
    twin = [(i, i ^ 1) for i in range(D)]

    base, out = first_product(h, heads)
    v = base
    for step in range(1, G):
        got = lax.all_to_all(out, ("layer", "plane"), 0, 0, axis_index_groups=pair_groups(step))
        other = lax.ppermute(got, "plane", twin)
        behind = v
        if step == 2:
            behind = wavenum = wave(heads, coef, mode_panel.reshape(MODES, 256), v)
        if step == 5:
            y, low, high, last = fronts_of(gathered, h, v)
            behind = last
        if step == 6:
            low, high, last, _ = lax.optimization_barrier((low, high, last, v))
            before = shift(high, "plane", 1)
            after = shift(low, "plane", -1)
            below = shift(last, "layer", 1)
        half = own_half(core, h, got, behind)
        mine = (group == step).astype(jnp.int32).reshape(1)
        v, out = other_half(core, mine, h, other, half, base, v)

    vb = v.astype(bf16)
    nl = shift(vb, "layer", -1)
    vl = shift(jnp.concatenate([vb[:, NY : 2 * NY], vb[:, 3 * NY :]], axis=1), "plane", 1)
    vh = shift(jnp.concatenate([vb[:, :NY], vb[:, 2 * NY : 3 * NY]], axis=1), "plane", -1)
    sol, res = residual(y, flat, before, after, below, v, nl, vl, vh, wavenum)
    return sol.reshape(rhs.shape), res.reshape(rhs.shape)


def solution(mesh):
    return jax.shard_map(
        shards,
        mesh=mesh,
        in_specs=(
            P(None, None, "layer", "plane", None),
            P("layer", None, "plane", None, None, None, None),
            P(None, "plane", None),
            P("plane", "layer"),
            P(),
            P(),
            P(),
        ),
        out_specs=(P(None, None, "layer", "plane", None), P(None, None, "layer", "plane", None)),
        check_vma=False,
    )
```

```python
import jax
import jax.numpy as jnp
from jax import lax
from jax.experimental import pallas as pl
from jax.experimental.pallas import tpu as pltpu
from jax.sharding import PartitionSpec as P

MODES = 256
NPTS = 32768
COUPLING = 0.8
ABSORB_RATE = 0.3
WAVE_SCALE = 0.8

G = 8
D = 16
C = 8
LZ = 96
R = 8
K = 512
NY = 128

bf16 = jnp.bfloat16
f32 = jnp.float32
VMEM = pltpu.VMEM


def whole(space=VMEM):
    return pl.BlockSpec(memory_space=space)


def params(mib):
    return pltpu.CompilerParams(vmem_limit_bytes=mib * 2**20)


def dot_t(x, h):
    return lax.dot_general(x, h, (((1,), (1,)), ((), ())), preferred_element_type=f32)


def prepare_kernel(rhs_ref, profile_ref, x_ref, chunk_ref):
    chunk_ref[0] = jnp.zeros((32, K), bf16)
    for a in range(2):
        for x in range(2):
            cols = pl.ds(a * 256 + x * NY, NY)
            for r in range(R):
                x_ref[pl.ds(r * LZ, LZ), cols] = rhs_ref[a, r, pl.ds(x, LZ, stride=2), :].astype(bf16)
    head = jnp.concatenate([rhs_ref[a, :, x, :] for a in range(2) for x in range(2)], axis=1)
    profile = jnp.concatenate([profile_ref[...], jnp.zeros((16, K - LZ), bf16)], axis=1)
    chunk = jnp.concatenate([head, jnp.zeros((8, K), f32)], axis=0).astype(bf16)
    for i in range(D):
        chunk_ref[i, pl.ds(0, 16), :] = chunk
        chunk_ref[i, pl.ds(16, 16), :] = profile


def prepare(rhs, profile):
    return pl.pallas_call(
        prepare_kernel,
        out_shape=(jax.ShapeDtypeStruct((R * LZ, K), bf16), jax.ShapeDtypeStruct((D, 32, K), bf16)),
        in_specs=[whole(), whole()],
        out_specs=(whole(), whole()),
        compiler_params=params(8),
    )(rhs, profile)


def arrange_kernel(blocks_ref, h_ref, in_buf, out_buf, in_sem, out_sem):
    m = lax.broadcasted_iota(jnp.int32, (256, 256), 0)
    n = lax.broadcasted_iota(jnp.int32, (256, 256), 1)
    swap = ((m // 16 == n % 16) & (m % 16 == n // 16)).astype(f32).astype(bf16)

    def rows(i):
        return pl.ds(pl.multiple_of(i * 32, 32), 32)

    def load(i):
        return pltpu.make_async_copy(blocks_ref.at[rows(i)], in_buf.at[i], in_sem.at[i])

    def store(i):
        return pltpu.make_async_copy(out_buf.at[:, :, rows(i)], h_ref.at[:, :, rows(i)], out_sem.at[i])

    for i in range(K // 32):
        load(i).start()

    @pl.loop(0, K // 32)
    def _(i):
        load(i).wait()
        for s in range(2):
            for half in range(2):
                tile = jnp.concatenate(
                    [in_buf[i, pl.ds(s * 16, 16), c, pl.ds(half * 16, 16), :].reshape(256, NY) for c in range(2)], axis=1
                )
                moved = jnp.dot(swap, tile, preferred_element_type=f32).astype(bf16)
                for q in range(16):
                    p = half * 16 + q
                    source = p // 2
                    into = pl.ds(pl.multiple_of(i * 32 + s * 16, 16), 16)
                    for c in range(2):
                        out_buf[source % 2, source // 2, into, pl.ds(c * 256 + (p % 2) * NY, NY)] = moved[
                            q * 16 : (q + 1) * 16, c * NY : (c + 1) * NY
                        ]
        store(i).start()

    for i in range(K // 32):
        store(i).wait()


def arrange(blocks):
    return pl.pallas_call(
        arrange_kernel,
        out_shape=jax.ShapeDtypeStruct((2, C, K, K), bf16),
        in_specs=[whole(pltpu.HBM)],
        out_specs=whole(pltpu.HBM),
        scratch_shapes=[
            VMEM((K // 32, 32, 2, 32, NY), bf16),
            VMEM((2, C, K, K), bf16),
            pltpu.SemaphoreType.DMA((K // 32,)),
            pltpu.SemaphoreType.DMA((K // 32,)),
        ],
        compiler_params=params(50),
        cost_estimate=pl.CostEstimate(flops=4 * 10**9, bytes_accessed=17 * 10**6, transcendentals=0),
    )(blocks)


COST = pl.CostEstimate(flops=10**8, bytes_accessed=5 * 10**6, transcendentals=0)


def fetch(h_ref, buf, sem, core):
    copies = [pltpu.make_async_copy(h_ref.at[core, k], buf.at[k], sem.at[k]) for k in range(C)]
    for copy in copies:
        copy.start()
    return copies


def first_kernel(h_ref, x_ref, v_ref, out_ref, even, odd, even_sem, odd_sem):
    bufs = (even, odd)
    copies = [fetch(h_ref, bufs[core], (even_sem, odd_sem)[core], core) for core in range(2)]
    acc = jnp.zeros((16, K), f32)
    for core in range(2):
        for k in range(C):
            copies[core][k].wait()
            acc = acc + dot_t(x_ref[2 * k + core, pl.ds(0, 16), :], bufs[core][k])
    v = acc[:R]
    v_ref[...] = v
    for i in range(D):
        out_ref[i] = v.astype(bf16)


HALF = [VMEM((C, K, K), bf16)]
SEMS = [pltpu.SemaphoreType.DMA((C,))]


def first_product(h, x):
    return pl.pallas_call(
        first_kernel,
        out_shape=MATVEC_OUT,
        in_specs=[whole(pltpu.HBM), whole()],
        out_specs=(whole(), whole()),
        scratch_shapes=HALF * 2 + SEMS * 2,
        compiler_params=params(50),
        cost_estimate=COST,
    )(h, x)


def own_kernel(core_ref, h_ref, x_ref, acc_ref, buf, sem):
    acc = jnp.zeros((R, K), f32)
    for k, copy in enumerate(fetch(h_ref, buf, sem, core_ref[0])):
        copy.wait()
        acc = acc + dot_t(x_ref[k], buf[k])
    acc_ref[...] = acc


def own_half(core, h, x):
    return pl.pallas_call(
        own_kernel,
        out_shape=jax.ShapeDtypeStruct((R, K), f32),
        in_specs=[whole(pltpu.SMEM), whole(pltpu.HBM), whole()],
        out_specs=whole(),
        scratch_shapes=HALF + SEMS,
        compiler_params=params(50),
        cost_estimate=COST,
    )(core, h, x)


def other_kernel(core_ref, mine_ref, h_ref, x_ref, half_ref, base_ref, old_ref, v_ref, out_ref, buf, sem):
    acc = half_ref[...]
    for k, copy in enumerate(fetch(h_ref, buf, sem, 1 - core_ref[0])):
        copy.wait()
        acc = acc + dot_t(x_ref[k], buf[k])
    v = jnp.where(mine_ref[0] > 0, base_ref[...] + COUPLING * acc, old_ref[...])
    v_ref[...] = v
    for i in range(D):
        out_ref[i] = v.astype(bf16)


MATVEC_OUT = (jax.ShapeDtypeStruct((R, K), f32), jax.ShapeDtypeStruct((D, R, K), bf16))


def other_half(core, mine, h, x, half, base, old):
    return pl.pallas_call(
        other_kernel,
        out_shape=MATVEC_OUT,
        in_specs=[whole(pltpu.SMEM)] * 2 + [whole(pltpu.HBM)] + [whole()] * 4,
        out_specs=(whole(), whole()),
        scratch_shapes=HALF + SEMS,
        compiler_params=params(50),
        cost_estimate=COST,
    )(core, mine, h, x, half, base, old)


def fronts_kernel(x_ref, h_ref, behind_ref, y_ref, low_ref, high_ref, last_ref, x_buf, h_buf, x_sem, h_sem):
    def loads(i):
        return (
            pltpu.make_async_copy(x_ref.at[i], x_buf.at[i], x_sem.at[i]),
            pltpu.make_async_copy(h_ref.at[lax.rem(i, 2), lax.div(i, 2)], h_buf.at[i], h_sem.at[i]),
        )

    @pl.loop(0, D)
    def _(i):
        for copy in loads(i):
            copy.start()

    y_ref[...] = jnp.zeros((R, LZ, K), f32)

    @pl.loop(0, D)
    def _(i):
        for copy in loads(i):
            copy.wait()
        for part in range(4):
            rows = pl.ds(part * 2 * LZ, 2 * LZ)
            y_ref[pl.ds(2 * part, 2)] += dot_t(x_buf[i, rows, :], h_buf[i]).reshape(2, LZ, K)

    for r in range(R):
        for a in range(2):
            low_ref[r, a] = y_ref[r, :, a * 256 : a * 256 + NY].astype(bf16)
            high_ref[r, a] = y_ref[r, :, a * 256 + NY : a * 256 + 256].astype(bf16)
    last_ref[...] = jnp.concatenate([y_ref[r, LZ - 1 : LZ, :] for r in range(R)], axis=0).astype(bf16)


def fronts_of(x, h, behind):
    halo = jax.ShapeDtypeStruct((R, 2, LZ, NY), bf16)
    return pl.pallas_call(
        fronts_kernel,
        out_shape=(jax.ShapeDtypeStruct((R, LZ, K), f32), halo, halo, jax.ShapeDtypeStruct((R, K), bf16)),
        in_specs=[whole(pltpu.HBM), whole(pltpu.HBM), whole(pl.ANY)],
        out_specs=(whole(),) * 4,
        scratch_shapes=[
            VMEM((D, R * LZ, K), bf16),
            VMEM((D, K, K), bf16),
            pltpu.SemaphoreType.DMA((D,)),
            pltpu.SemaphoreType.DMA((D,)),
        ],
        compiler_params=params(50),
        cost_estimate=pl.CostEstimate(flops=6 * 10**9, bytes_accessed=23 * 10**6, transcendentals=0),
    )(x, h, behind)


def wave_kernel(x_ref, coef_ref, panel_ref, behind_ref, out_ref):
    profile = jnp.concatenate([x_ref[i, pl.ds(16, 16), :][:, :LZ] for i in range(D)], axis=0).astype(f32)
    panel = panel_ref[...]
    for r in range(R):
        weights = profile * coef_ref[:, r : r + 1]
        log = jnp.zeros((LZ, 256), f32)
        for _ in range(3):
            term = weights.astype(bf16)
            weights = weights - term.astype(f32)
            log = log + lax.dot_general(term, panel, (((0,), (0,)), ((), ())), preferred_element_type=f32)
        out_ref[r] = WAVE_SCALE * jnp.exp(-2.0 * log)


def wave(x, coef, panel, behind):
    return pl.pallas_call(
        wave_kernel,
        out_shape=jax.ShapeDtypeStruct((R, LZ, 256), f32),
        in_specs=[whole()] * 3 + [whole(pl.ANY)],
        out_specs=whole(),
        compiler_params=params(8),
        cost_estimate=pl.CostEstimate(flops=3 * 10**8, bytes_accessed=2 * 10**6, transcendentals=2 * 10**5),
    )(x, coef, panel, behind)


def residual_kernel(y_ref, rhs_ref, low_ref, high_ref, prev_ref, v_ref, nl_ref, vl_ref, vh_ref, wave_ref, sol_ref, res_ref):
    row = lax.broadcasted_iota(jnp.int32, (LZ, NY), 0)
    lane = lax.broadcasted_iota(jnp.int32, (LZ, NY), 1)
    for r in range(R):
        s = {}
        for a in range(2):
            for x in range(2):
                cols = slice(a * 256 + x * NY, a * 256 + (x + 1) * NY)
                s[a, x] = jnp.where(row == 0, v_ref[r : r + 1, cols], y_ref[r, :, cols])
        lap = {}
        for a in range(2):
            below = jnp.where(row == 0, vl_ref[r : r + 1, a * NY : (a + 1) * NY].astype(f32), low_ref[r, a].astype(f32))
            above = jnp.where(row == 0, vh_ref[r : r + 1, a * NY : (a + 1) * NY].astype(f32), high_ref[r, a].astype(f32))
            for x in range(2):
                cols = slice(a * 256 + x * NY, a * 256 + (x + 1) * NY)
                own = s[a, x]
                before = jnp.where(row == 0, prev_ref[r : r + 1, cols].astype(f32), pltpu.roll(own, 1, 0))
                after = jnp.where(row == LZ - 1, nl_ref[r : r + 1, cols].astype(f32), pltpu.roll(own, LZ - 1, 0))
                left = jnp.where(lane == 0, 0.0, pltpu.roll(own, 1, 1))
                right = jnp.where(lane == NY - 1, 0.0, pltpu.roll(own, NY - 1, 1))
                beside = before + after + left + right
                beside = beside + (below if x == 0 else s[a, 0]) + (s[a, 1] if x == 0 else above)
                lap[a, x] = 6.0 * own - beside
        for x in range(2):
            w = wave_ref[r, :, x * NY : (x + 1) * NY]
            rows = pl.ds(x, LZ, stride=2)
            real = lap[0, x] - w * s[0, x] + ABSORB_RATE * w * s[1, x]
            imag = lap[1, x] - w * s[1, x] - ABSORB_RATE * w * s[0, x]
            sol_ref[0, r, rows, :] = s[0, x]
            sol_ref[1, r, rows, :] = s[1, x]
            res_ref[0, r, rows, :] = rhs_ref[0, r, rows, :] - real
            res_ref[1, r, rows, :] = rhs_ref[1, r, rows, :] - imag


def residual(*args):
    shape = jax.ShapeDtypeStruct((2, R, 2 * LZ, NY), f32)
    return pl.pallas_call(
        residual_kernel,
        out_shape=(shape, shape),
        in_specs=[whole()] * len(args),
        out_specs=(whole(), whole()),
        compiler_params=params(24),
    )(*args)


def pair_groups(step):
    groups = []
    for k in range(G // 2):
        first = (2 * k + step - 1) % G
        second = (first + 1) % G
        for core in range(2):
            groups.append([g * D + 2 * i + core for g in (first, second) for i in range(C)])
    return groups


def shift(value, axis, by):
    size = lax.axis_size(axis)
    return lax.ppermute(value, axis, [(i, i + by) for i in range(size) if 0 <= i + by < size])


def shards(rhs, inverse_blocks, mode_panel, mode_profile, generator, lattice_index, shift_index):
    group = lax.axis_index("layer")
    flat = rhs.reshape(2, R, 2 * LZ, NY)
    own, chunk = prepare(flat, mode_profile)
    gathered = lax.all_gather(own, "plane", axis=0)
    heads = lax.all_to_all(chunk, "plane", 0, 0)
    h = arrange(inverse_blocks.reshape(K, 2, 32, NY))

    mixed = (lattice_index[None, :] * generator[:, None] + shift_index.T) % NPTS
    amplitude = 0.25 / jnp.sqrt(1.0 + jnp.arange(MODES, dtype=f32) / 8.0)
    coef = amplitude[:, None] * ((mixed.astype(f32) + 0.5) / NPTS - 0.5)
    core = lax.rem(lax.axis_index("plane"), 2).astype(jnp.int32).reshape(1)
    twin = [(i, i ^ 1) for i in range(D)]

    base, out = first_product(h, heads)
    v = base
    for step in range(1, G):
        got = lax.all_to_all(out, ("layer", "plane"), 0, 0, axis_index_groups=pair_groups(step))
        if step == 2:
            wavenum = wave(heads, coef, mode_panel.reshape(MODES, 256), v)
            got, wavenum = lax.optimization_barrier((got, wavenum))
        if step == 5:
            y, low, high, last = fronts_of(gathered, h, v)
            got, low, high, last = lax.optimization_barrier((got, low, high, last))
        if step == 6:
            low, high, last, v = lax.optimization_barrier((low, high, last, v))
            before = shift(high, "plane", 1)
            after = shift(low, "plane", -1)
            below = shift(last, "layer", 1)
            got, before, after, below = lax.optimization_barrier((got, before, after, below))
        other = lax.ppermute(got, "plane", twin)
        half = own_half(core, h, got)
        mine = (group == step).astype(jnp.int32).reshape(1)
        v, out = other_half(core, mine, h, other, half, base, v)

    vb = v.astype(bf16)
    nl = shift(vb, "layer", -1)
    vl = shift(jnp.concatenate([vb[:, NY : 2 * NY], vb[:, 3 * NY :]], axis=1), "plane", 1)
    vh = shift(jnp.concatenate([vb[:, :NY], vb[:, 2 * NY : 3 * NY]], axis=1), "plane", -1)
    sol, res = residual(y, flat, before, after, below, v, nl, vl, vh, wavenum)
    return sol.reshape(rhs.shape), res.reshape(rhs.shape)


def solution(mesh):
    return jax.shard_map(
        shards,
        mesh=mesh,
        in_specs=(
            P(None, None, "layer", "plane", None),
            P("layer", None, "plane", None, None, None, None),
            P(None, "plane", None),
            P("plane", "layer"),
            P(),
            P(),
            P(),
        ),
        out_specs=(P(None, None, "layer", "plane", None), P(None, None, "layer", "plane", None)),
        check_vma=False,
    )
```

```python
import jax
import jax.numpy as jnp
from jax import lax
from jax.experimental import pallas as pl
from jax.experimental.pallas import tpu as pltpu
from jax.sharding import PartitionSpec as P

MODES = 256
NPTS = 32768
COUPLING = 0.8
ABSORB_RATE = 0.3
WAVE_SCALE = 0.8

G = 8
D = 16
C = 8
LZ = 96
R = 8
K = 512
NY = 128

bf16 = jnp.bfloat16
f32 = jnp.float32
VMEM = pltpu.VMEM


def whole(space=VMEM):
    return pl.BlockSpec(memory_space=space)


def params(mib):
    return pltpu.CompilerParams(vmem_limit_bytes=mib * 2**20)


def dot_t(x, h):
    return lax.dot_general(x, h, (((1,), (1,)), ((), ())), preferred_element_type=f32)


def prepare_kernel(rhs_ref, profile_ref, x_ref, chunk_ref):
    chunk_ref[0] = jnp.zeros((32, K), bf16)
    for a in range(2):
        for x in range(2):
            cols = pl.ds(a * 256 + x * NY, NY)
            for r in range(R):
                x_ref[pl.ds(r * LZ, LZ), cols] = rhs_ref[a, r, pl.ds(x, LZ, stride=2), :].astype(bf16)
    head = jnp.concatenate([rhs_ref[a, :, x, :] for a in range(2) for x in range(2)], axis=1)
    profile = jnp.concatenate([profile_ref[...], jnp.zeros((16, K - LZ), bf16)], axis=1)
    chunk = jnp.concatenate([head, jnp.zeros((8, K), f32)], axis=0).astype(bf16)
    for i in range(D):
        chunk_ref[i, pl.ds(0, 16), :] = chunk
        chunk_ref[i, pl.ds(16, 16), :] = profile


def prepare(rhs, profile):
    return pl.pallas_call(
        prepare_kernel,
        out_shape=(jax.ShapeDtypeStruct((R * LZ, K), bf16), jax.ShapeDtypeStruct((D, 32, K), bf16)),
        in_specs=[whole(), whole()],
        out_specs=(whole(), whole()),
        compiler_params=params(8),
    )(rhs, profile)


def arrange_kernel(blocks_ref, h_ref, in_buf, out_buf, in_sem, out_sem):
    m = lax.broadcasted_iota(jnp.int32, (256, 256), 0)
    n = lax.broadcasted_iota(jnp.int32, (256, 256), 1)
    swap = ((m // 16 == n % 16) & (m % 16 == n // 16)).astype(f32).astype(bf16)

    def rows(i):
        return pl.ds(pl.multiple_of(i * 32, 32), 32)

    def load(i):
        return pltpu.make_async_copy(blocks_ref.at[rows(i)], in_buf.at[i], in_sem.at[i])

    def store(i):
        return pltpu.make_async_copy(out_buf.at[:, :, rows(i)], h_ref.at[:, :, rows(i)], out_sem.at[i])

    for i in range(K // 32):
        load(i).start()

    @pl.loop(0, K // 32)
    def _(i):
        load(i).wait()
        for s in range(2):
            for half in range(2):
                tile = jnp.concatenate(
                    [in_buf[i, pl.ds(s * 16, 16), c, pl.ds(half * 16, 16), :].reshape(256, NY) for c in range(2)], axis=1
                )
                moved = jnp.dot(swap, tile, preferred_element_type=f32).astype(bf16)
                for q in range(16):
                    p = half * 16 + q
                    source = p // 2
                    into = pl.ds(pl.multiple_of(i * 32 + s * 16, 16), 16)
                    for c in range(2):
                        out_buf[source % 2, source // 2, into, pl.ds(c * 256 + (p % 2) * NY, NY)] = moved[
                            q * 16 : (q + 1) * 16, c * NY : (c + 1) * NY
                        ]
        store(i).start()

    for i in range(K // 32):
        store(i).wait()


def arrange(blocks):
    return pl.pallas_call(
        arrange_kernel,
        out_shape=jax.ShapeDtypeStruct((2, C, K, K), bf16),
        in_specs=[whole(pltpu.HBM)],
        out_specs=whole(pltpu.HBM),
        scratch_shapes=[
            VMEM((K // 32, 32, 2, 32, NY), bf16),
            VMEM((2, C, K, K), bf16),
            pltpu.SemaphoreType.DMA((K // 32,)),
            pltpu.SemaphoreType.DMA((K // 32,)),
        ],
        compiler_params=params(50),
        cost_estimate=pl.CostEstimate(flops=4 * 10**9, bytes_accessed=17 * 10**6, transcendentals=0),
    )(blocks)


COST = pl.CostEstimate(flops=10**8, bytes_accessed=5 * 10**6, transcendentals=0)


def fetch(h_ref, buf, sem, core):
    copies = [pltpu.make_async_copy(h_ref.at[core, k], buf.at[k], sem.at[k]) for k in range(C)]
    for copy in copies:
        copy.start()
    return copies


def first_kernel(h_ref, x_ref, v_ref, out_ref, even, odd, even_sem, odd_sem):
    bufs = (even, odd)
    copies = [fetch(h_ref, bufs[core], (even_sem, odd_sem)[core], core) for core in range(2)]
    acc = jnp.zeros((16, K), f32)
    for core in range(2):
        for k in range(C):
            copies[core][k].wait()
            acc = acc + dot_t(x_ref[2 * k + core, pl.ds(0, 16), :], bufs[core][k])
    v = acc[:R]
    v_ref[...] = v
    for i in range(D):
        out_ref[i] = v.astype(bf16)


HALF = [VMEM((C, K, K), bf16)]
SEMS = [pltpu.SemaphoreType.DMA((C,))]


def first_product(h, x):
    return pl.pallas_call(
        first_kernel,
        out_shape=MATVEC_OUT,
        in_specs=[whole(pltpu.HBM), whole()],
        out_specs=(whole(), whole()),
        scratch_shapes=HALF * 2 + SEMS * 2,
        compiler_params=params(50),
        cost_estimate=COST,
    )(h, x)


def own_kernel(core_ref, h_ref, x_ref, acc_ref, buf, sem):
    acc = jnp.zeros((R, K), f32)
    for k, copy in enumerate(fetch(h_ref, buf, sem, core_ref[0])):
        copy.wait()
        acc = acc + dot_t(x_ref[k], buf[k])
    acc_ref[...] = acc


def own_half(core, h, x):
    return pl.pallas_call(
        own_kernel,
        out_shape=jax.ShapeDtypeStruct((R, K), f32),
        in_specs=[whole(pltpu.SMEM), whole(pltpu.HBM), whole()],
        out_specs=whole(),
        scratch_shapes=HALF + SEMS,
        compiler_params=params(50),
        cost_estimate=COST,
    )(core, h, x)


def other_kernel(core_ref, mine_ref, h_ref, x_ref, half_ref, base_ref, old_ref, v_ref, out_ref, buf, sem):
    acc = half_ref[...]
    for k, copy in enumerate(fetch(h_ref, buf, sem, 1 - core_ref[0])):
        copy.wait()
        acc = acc + dot_t(x_ref[k], buf[k])
    v = jnp.where(mine_ref[0] > 0, base_ref[...] + COUPLING * acc, old_ref[...])
    v_ref[...] = v
    for i in range(D):
        out_ref[i] = v.astype(bf16)


MATVEC_OUT = (jax.ShapeDtypeStruct((R, K), f32), jax.ShapeDtypeStruct((D, R, K), bf16))


def other_half(core, mine, h, x, half, base, old):
    return pl.pallas_call(
        other_kernel,
        out_shape=MATVEC_OUT,
        in_specs=[whole(pltpu.SMEM)] * 2 + [whole(pltpu.HBM)] + [whole()] * 4,
        out_specs=(whole(), whole()),
        scratch_shapes=HALF + SEMS,
        compiler_params=params(50),
        cost_estimate=COST,
    )(core, mine, h, x, half, base, old)


def fronts_kernel(x_ref, h_ref, behind_ref, y_ref, low_ref, high_ref, last_ref, x_buf, h_buf, x_sem, h_sem):
    def loads(i):
        core, chip = lax.rem(lax.div(i, 2), 2), lax.div(i, 4) * 2 + lax.rem(i, 2)
        return (
            pltpu.make_async_copy(x_ref.at[i], x_buf.at[i], x_sem.at[i]),
            pltpu.make_async_copy(h_ref.at[core, chip], h_buf.at[i], h_sem.at[i]),
        )

    @pl.loop(0, D)
    def _(i):
        for copy in loads(i):
            copy.start()

    y_ref[...] = jnp.zeros((R, LZ, K), f32)

    @pl.loop(0, D // 2)
    def _(j):
        for i in (2 * j, 2 * j + 1):
            for copy in loads(i):
                copy.wait()
        total = dot_t(x_buf[2 * j], h_buf[2 * j]) + dot_t(x_buf[2 * j + 1], h_buf[2 * j + 1])
        y_ref[...] += total.reshape(R, LZ, K)

    for r in range(R):
        for a in range(2):
            low_ref[r, a] = y_ref[r, :, a * 256 : a * 256 + NY].astype(bf16)
            high_ref[r, a] = y_ref[r, :, a * 256 + NY : a * 256 + 256].astype(bf16)
    last_ref[...] = jnp.concatenate([y_ref[r, LZ - 1 : LZ, :] for r in range(R)], axis=0).astype(bf16)


def fronts_of(x, h, behind):
    halo = jax.ShapeDtypeStruct((R, 2, LZ, NY), bf16)
    return pl.pallas_call(
        fronts_kernel,
        out_shape=(jax.ShapeDtypeStruct((R, LZ, K), f32), halo, halo, jax.ShapeDtypeStruct((R, K), bf16)),
        in_specs=[whole(pltpu.HBM), whole(pltpu.HBM), whole(pl.ANY)],
        out_specs=(whole(),) * 4,
        scratch_shapes=[
            VMEM((D, R * LZ, K), bf16),
            VMEM((D, K, K), bf16),
            pltpu.SemaphoreType.DMA((D,)),
            pltpu.SemaphoreType.DMA((D,)),
        ],
        compiler_params=params(50),
        cost_estimate=pl.CostEstimate(flops=6 * 10**9, bytes_accessed=23 * 10**6, transcendentals=0),
    )(x, h, behind)


def gate_kernel(*refs):
    pass


def gate(behind, *arrays):
    n = len(arrays)
    return pl.pallas_call(
        gate_kernel,
        out_shape=tuple(jax.ShapeDtypeStruct(x.shape, x.dtype) for x in arrays),
        in_specs=[whole(pl.ANY)] * (n + 1),
        out_specs=(whole(pl.ANY),) * n,
        input_output_aliases={i: i for i in range(n)},
        compiler_params=params(8),
        cost_estimate=pl.CostEstimate(flops=6 * 10**9, bytes_accessed=10**6, transcendentals=0),
    )(*arrays, behind)


def wave_kernel(x_ref, coef_ref, panel_ref, behind_ref, out_ref):
    profile = jnp.concatenate([x_ref[i, pl.ds(16, 16), :][:, :LZ] for i in range(D)], axis=0).astype(f32)
    panel = panel_ref[...]
    for r in range(R):
        weights = profile * coef_ref[:, r : r + 1]
        log = jnp.zeros((LZ, 256), f32)
        for _ in range(3):
            term = weights.astype(bf16)
            weights = weights - term.astype(f32)
            log = log + lax.dot_general(term, panel, (((0,), (0,)), ((), ())), preferred_element_type=f32)
        out_ref[r] = WAVE_SCALE * jnp.exp(-2.0 * log)


def wave(x, coef, panel, behind):
    return pl.pallas_call(
        wave_kernel,
        out_shape=jax.ShapeDtypeStruct((R, LZ, 256), f32),
        in_specs=[whole()] * 3 + [whole(pl.ANY)],
        out_specs=whole(),
        compiler_params=params(8),
        cost_estimate=pl.CostEstimate(flops=3 * 10**8, bytes_accessed=2 * 10**6, transcendentals=2 * 10**5),
    )(x, coef, panel, behind)


def residual_kernel(y_ref, rhs_ref, low_ref, high_ref, prev_ref, v_ref, nl_ref, vl_ref, vh_ref, wave_ref, sol_ref, res_ref):
    row = lax.broadcasted_iota(jnp.int32, (LZ, NY), 0)
    lane = lax.broadcasted_iota(jnp.int32, (LZ, NY), 1)
    for r in range(R):
        s = {}
        for a in range(2):
            for x in range(2):
                cols = slice(a * 256 + x * NY, a * 256 + (x + 1) * NY)
                s[a, x] = jnp.where(row == 0, v_ref[r : r + 1, cols], y_ref[r, :, cols])
        lap = {}
        for a in range(2):
            below = jnp.where(row == 0, vl_ref[r : r + 1, a * NY : (a + 1) * NY].astype(f32), low_ref[r, a].astype(f32))
            above = jnp.where(row == 0, vh_ref[r : r + 1, a * NY : (a + 1) * NY].astype(f32), high_ref[r, a].astype(f32))
            for x in range(2):
                cols = slice(a * 256 + x * NY, a * 256 + (x + 1) * NY)
                own = s[a, x]
                before = jnp.where(row == 0, prev_ref[r : r + 1, cols].astype(f32), pltpu.roll(own, 1, 0))
                after = jnp.where(row == LZ - 1, nl_ref[r : r + 1, cols].astype(f32), pltpu.roll(own, LZ - 1, 0))
                left = jnp.where(lane == 0, 0.0, pltpu.roll(own, 1, 1))
                right = jnp.where(lane == NY - 1, 0.0, pltpu.roll(own, NY - 1, 1))
                beside = before + after + left + right
                beside = beside + (below if x == 0 else s[a, 0]) + (s[a, 1] if x == 0 else above)
                lap[a, x] = 6.0 * own - beside
        for x in range(2):
            w = wave_ref[r, :, x * NY : (x + 1) * NY]
            rows = pl.ds(x, LZ, stride=2)
            real = lap[0, x] - w * s[0, x] + ABSORB_RATE * w * s[1, x]
            imag = lap[1, x] - w * s[1, x] - ABSORB_RATE * w * s[0, x]
            sol_ref[0, r, rows, :] = s[0, x]
            sol_ref[1, r, rows, :] = s[1, x]
            res_ref[0, r, rows, :] = rhs_ref[0, r, rows, :] - real
            res_ref[1, r, rows, :] = rhs_ref[1, r, rows, :] - imag


def residual(*args):
    shape = jax.ShapeDtypeStruct((2, R, 2 * LZ, NY), f32)
    return pl.pallas_call(
        residual_kernel,
        out_shape=(shape, shape),
        in_specs=[whole()] * len(args),
        out_specs=(whole(), whole()),
        compiler_params=params(24),
    )(*args)


def pair_groups(step):
    groups = []
    for k in range(G // 2):
        first = (2 * k + step - 1) % G
        second = (first + 1) % G
        for core in range(2):
            groups.append([g * D + 2 * i + core for g in (first, second) for i in range(C)])
    return groups


def shift(value, axis, by):
    size = lax.axis_size(axis)
    return lax.ppermute(value, axis, [(i, i + by) for i in range(size) if 0 <= i + by < size])


def shards(rhs, inverse_blocks, mode_panel, mode_profile, generator, lattice_index, shift_index):
    group = lax.axis_index("layer")
    flat = rhs.reshape(2, R, 2 * LZ, NY)
    own, chunk = prepare(flat, mode_profile)
    along_x = [[z * 4 + x * 2 + c for x in range(2)] for z in range(4) for c in range(2)]
    along_z = [[z * 4 + x * 2 + c for z in range(4) for c in range(2)] for x in range(2)]
    paired = lax.all_gather(own, "plane", axis=0, axis_index_groups=along_x)
    heads = lax.all_to_all(chunk, "plane", 0, 0)
    h = arrange(inverse_blocks.reshape(K, 2, 32, NY))

    mixed = (lattice_index[None, :] * generator[:, None] + shift_index.T) % NPTS
    amplitude = 0.25 / jnp.sqrt(1.0 + jnp.arange(MODES, dtype=f32) / 8.0)
    coef = amplitude[:, None] * ((mixed.astype(f32) + 0.5) / NPTS - 0.5)
    core = lax.rem(lax.axis_index("plane"), 2).astype(jnp.int32).reshape(1)
    twin = [(i, i ^ 1) for i in range(D)]

    base, out = first_product(h, heads)
    v = base
    for step in range(1, G):
        if step == 2:
            paired, _ = lax.optimization_barrier((paired, v))
            gathered = lax.all_gather(paired, "plane", axis=0, axis_index_groups=along_z).reshape(D, R * LZ, K)
        got = lax.all_to_all(out, ("layer", "plane"), 0, 0, axis_index_groups=pair_groups(step))
        if step == 2:
            wavenum = wave(heads, coef, mode_panel.reshape(MODES, 256), v)
            got, wavenum = lax.optimization_barrier((got, wavenum))
        if step == 6:
            y, low, high, last = fronts_of(gathered, h, v)
            got, low, high, last = lax.optimization_barrier((got, low, high, last))
        if step == 7:
            low, high, last = gate(v, low, high, last)
            before = shift(high, "plane", 1)
            after = shift(low, "plane", -1)
            below = shift(last, "layer", 1)
            got, before, after, below = lax.optimization_barrier((got, before, after, below))
        other = lax.ppermute(got, "plane", twin)
        half = own_half(core, h, got)
        mine = (group == step).astype(jnp.int32).reshape(1)
        v, out = other_half(core, mine, h, other, half, base, v)

    vb = v.astype(bf16)
    nl = shift(vb, "layer", -1)
    vl = shift(jnp.concatenate([vb[:, NY : 2 * NY], vb[:, 3 * NY :]], axis=1), "plane", 1)
    vh = shift(jnp.concatenate([vb[:, :NY], vb[:, 2 * NY : 3 * NY]], axis=1), "plane", -1)
    sol, res = residual(y, flat, before, after, below, v, nl, vl, vh, wavenum)
    return sol.reshape(rhs.shape), res.reshape(rhs.shape)


def solution(mesh):
    return jax.shard_map(
        shards,
        mesh=mesh,
        in_specs=(
            P(None, None, "layer", "plane", None),
            P("layer", None, "plane", None, None, None, None),
            P(None, "plane", None),
            P("plane", "layer"),
            P(),
            P(),
            P(),
        ),
        out_specs=(P(None, None, "layer", "plane", None), P(None, None, "layer", "plane", None)),
        check_vma=False,
    )
```

```python
import jax
import jax.numpy as jnp
from jax import lax
from jax.experimental import pallas as pl
from jax.experimental.pallas import tpu as pltpu
from jax.sharding import PartitionSpec as P

MODES = 256
NPTS = 32768
COUPLING = 0.8
ABSORB_RATE = 0.3
WAVE_SCALE = 0.8

G = 8
D = 16
C = 8
LZ = 96
R = 8
K = 512
NY = 128
KEEP = 4

bf16 = jnp.bfloat16
f32 = jnp.float32
VMEM = pltpu.VMEM


def whole(space=VMEM):
    return pl.BlockSpec(memory_space=space)


def params(mib):
    return pltpu.CompilerParams(vmem_limit_bytes=mib * 2**20)


def dot_t(x, h):
    return lax.dot_general(x, h, (((1,), (1,)), ((), ())), preferred_element_type=f32)


def prepare_kernel(rhs_ref, profile_ref, x_ref, chunk_ref):
    for a in range(2):
        for x in range(2):
            cols = pl.ds(a * 256 + x * NY, NY)
            for r in range(R):
                x_ref[pl.ds(r * LZ, LZ), cols] = rhs_ref[a, r, pl.ds(x, LZ, stride=2), :].astype(bf16)
    head = jnp.concatenate([rhs_ref[a, :, x, :] for a in range(2) for x in range(2)], axis=1)
    profile = profile_ref[...].astype(f32)
    gap = jnp.zeros((8, NY - LZ), f32)
    tail = jnp.concatenate([profile[:8], gap, profile[8:], gap, jnp.zeros((8, K - 2 * NY), f32)], axis=1)
    chunk = jnp.concatenate([head, tail], axis=0).astype(bf16)
    for i in range(D):
        chunk_ref[i] = chunk


def prepare(rhs, profile):
    return pl.pallas_call(
        prepare_kernel,
        out_shape=(jax.ShapeDtypeStruct((R * LZ, K), bf16), jax.ShapeDtypeStruct((D, 16, K), bf16)),
        in_specs=[whole(), whole()],
        out_specs=(whole(), whole()),
        compiler_params=params(8),
    )(rhs, profile)


def arrange_kernel(blocks_ref, h_ref, in_buf, out_buf, in_sem, out_sem):
    m = lax.broadcasted_iota(jnp.int32, (256, 256), 0)
    n = lax.broadcasted_iota(jnp.int32, (256, 256), 1)
    swap = ((m // 16 == n % 16) & (m % 16 == n // 16)).astype(f32).astype(bf16)

    def rows(i):
        return pl.ds(pl.multiple_of(i * 32, 32), 32)

    def load(i):
        return pltpu.make_async_copy(blocks_ref.at[rows(i)], in_buf.at[i], in_sem.at[i])

    def store(i):
        return pltpu.make_async_copy(out_buf.at[:, :, rows(i)], h_ref.at[:, :, rows(i)], out_sem.at[i])

    for i in range(K // 32):
        load(i).start()

    @pl.loop(0, K // 32)
    def _(i):
        load(i).wait()
        for s in range(2):
            for half in range(2):
                tile = jnp.concatenate(
                    [in_buf[i, pl.ds(s * 16, 16), c, pl.ds(half * 16, 16), :].reshape(256, NY) for c in range(2)], axis=1
                )
                moved = jnp.dot(swap, tile, preferred_element_type=f32).astype(bf16)
                for q in range(16):
                    p = half * 16 + q
                    source = p // 2
                    into = pl.ds(pl.multiple_of(i * 32 + s * 16, 16), 16)
                    for c in range(2):
                        out_buf[source % 2, source // 2, into, pl.ds(c * 256 + (p % 2) * NY, NY)] = moved[
                            q * 16 : (q + 1) * 16, c * NY : (c + 1) * NY
                        ]
        store(i).start()

    for i in range(K // 32):
        store(i).wait()


def arrange(blocks):
    return pl.pallas_call(
        arrange_kernel,
        out_shape=jax.ShapeDtypeStruct((2, C, K, K), bf16),
        in_specs=[whole(pltpu.HBM)],
        out_specs=whole(pltpu.HBM),
        scratch_shapes=[
            VMEM((K // 32, 32, 2, 32, NY), bf16),
            VMEM((2, C, K, K), bf16),
            pltpu.SemaphoreType.DMA((K // 32,)),
            pltpu.SemaphoreType.DMA((K // 32,)),
        ],
        compiler_params=params(50),
        cost_estimate=pl.CostEstimate(flops=4 * 10**9, bytes_accessed=17 * 10**6, transcendentals=0),
    )(blocks)


COST = pl.CostEstimate(flops=10**8, bytes_accessed=5 * 10**6, transcendentals=0)


def fetch(h_ref, buf, sem, core, first=0):
    copies = [pltpu.make_async_copy(h_ref.at[core, k], buf.at[k], sem.at[k]) for k in range(first, C)]
    for copy in copies:
        copy.start()
    return copies


def first_kernel(core_ref, h_ref, x_ref, v_ref, out_ref, keep_ref, even, odd, even_sem, odd_sem):
    bufs = (even, odd)
    copies = [fetch(h_ref, bufs[core], (even_sem, odd_sem)[core], core) for core in range(2)]
    acc = jnp.zeros((16, K), f32)
    for core in range(2):
        for k in range(C):
            copies[core][k].wait()
            acc = acc + dot_t(x_ref[2 * k + core], bufs[core][k])
    v = acc[:R]
    v_ref[...] = v
    for i in range(D):
        out_ref[i] = v.astype(bf16)
    for core in range(2):

        @pl.when(core_ref[0] == core)
        def _():
            for k in range(KEEP):
                keep_ref[k] = bufs[core][k]


HALF = [VMEM((C, K, K), bf16)]
SEMS = [pltpu.SemaphoreType.DMA((C,))]


def first_product(core, h, x):
    return pl.pallas_call(
        first_kernel,
        out_shape=MATVEC_OUT + (jax.ShapeDtypeStruct((KEEP, K, K), bf16),),
        in_specs=[whole(pltpu.SMEM), whole(pltpu.HBM), whole()],
        out_specs=(whole(),) * 3,
        scratch_shapes=HALF * 2 + SEMS * 2,
        compiler_params=params(50),
        cost_estimate=COST,
    )(core, h, x)


def own_kernel(core_ref, h_ref, keep_ref, x_ref, acc_ref, buf, sem):
    copies = fetch(h_ref, buf, sem, core_ref[0], KEEP)
    acc = jnp.zeros((R, K), f32)
    for k in range(KEEP):
        acc = acc + dot_t(x_ref[k], keep_ref[k])
    for k in range(KEEP, C):
        copies[k - KEEP].wait()
        acc = acc + dot_t(x_ref[k], buf[k])
    acc_ref[...] = acc


def own_half(core, h, keep, x):
    return pl.pallas_call(
        own_kernel,
        out_shape=jax.ShapeDtypeStruct((R, K), f32),
        in_specs=[whole(pltpu.SMEM), whole(pltpu.HBM), whole(), whole()],
        out_specs=whole(),
        scratch_shapes=HALF + SEMS,
        compiler_params=params(50),
        cost_estimate=COST,
    )(core, h, keep, x)


def other_kernel(core_ref, mine_ref, h_ref, x_ref, half_ref, base_ref, old_ref, v_ref, out_ref, buf, sem, ends_ref=None):
    acc = half_ref[...]
    for k, copy in enumerate(fetch(h_ref, buf, sem, 1 - core_ref[0])):
        copy.wait()
        acc = acc + dot_t(x_ref[k], buf[k])
    v = jnp.where(mine_ref[0] > 0, base_ref[...] + COUPLING * acc, old_ref[...])
    v_ref[...] = v
    rounded = v.astype(bf16)
    if ends_ref is None:
        for i in range(D):
            out_ref[i] = rounded
        return
    out_ref[...] = rounded
    low = jnp.concatenate([rounded[:, :NY], rounded[:, 2 * NY : 3 * NY]], axis=1)
    high = jnp.concatenate([rounded[:, NY : 2 * NY], rounded[:, 3 * NY :]], axis=1)
    odd = core_ref[0] > 0
    ends_ref[0] = jnp.where(odd, high, low)
    ends_ref[1] = jnp.where(odd, low, high)


def final_kernel(core_ref, mine_ref, h_ref, x_ref, half_ref, base_ref, old_ref, v_ref, out_ref, ends_ref, buf, sem):
    other_kernel(core_ref, mine_ref, h_ref, x_ref, half_ref, base_ref, old_ref, v_ref, out_ref, buf, sem, ends_ref)


MATVEC_OUT = (jax.ShapeDtypeStruct((R, K), f32), jax.ShapeDtypeStruct((D, R, K), bf16))


def other_half(core, mine, h, x, half, base, old, final):
    out = MATVEC_OUT
    if final:
        out = (out[0], jax.ShapeDtypeStruct((R, K), bf16), jax.ShapeDtypeStruct((2, R, 256), bf16))
    return pl.pallas_call(
        final_kernel if final else other_kernel,
        out_shape=out,
        in_specs=[whole(pltpu.SMEM)] * 2 + [whole(pltpu.HBM)] + [whole()] * 4,
        out_specs=(whole(),) * len(out),
        scratch_shapes=HALF + SEMS,
        compiler_params=params(50),
        cost_estimate=COST,
    )(core, mine, h, x, half, base, old)


def fronts_kernel(core_ref, x_ref, h_ref, behind_ref, y_ref, inner_ref, outer_ref, last_ref, x_buf, h_buf, x_sem, h_sem):
    def loads(i):
        core, chip = lax.rem(lax.div(i, 2), 2), lax.div(i, 4) * 2 + lax.rem(i, 2)
        return (
            pltpu.make_async_copy(x_ref.at[i], x_buf.at[i], x_sem.at[i]),
            pltpu.make_async_copy(h_ref.at[core, chip], h_buf.at[i], h_sem.at[i]),
        )

    @pl.loop(0, D)
    def _(i):
        for copy in loads(i):
            copy.start()

    y_ref[...] = jnp.zeros((R, LZ, K), f32)

    @pl.loop(0, D // 2)
    def _(j):
        for i in (2 * j, 2 * j + 1):
            for copy in loads(i):
                copy.wait()
        total = dot_t(x_buf[2 * j], h_buf[2 * j]) + dot_t(x_buf[2 * j + 1], h_buf[2 * j + 1])
        y_ref[...] += total.reshape(R, LZ, K)

    odd = core_ref[0] > 0
    for r in range(R):
        for a in range(2):
            low = y_ref[r, :, a * 256 : a * 256 + NY].astype(bf16)
            high = y_ref[r, :, a * 256 + NY : a * 256 + 256].astype(bf16)
            inner_ref[r, a] = jnp.where(odd, low, high)
            outer_ref[r, a] = jnp.where(odd, high, low)
    last_ref[...] = jnp.concatenate([y_ref[r, LZ - 1 : LZ, :] for r in range(R)], axis=0).astype(bf16)


def fronts_of(core, x, h, behind):
    halo = jax.ShapeDtypeStruct((R, 2, LZ, NY), bf16)
    return pl.pallas_call(
        fronts_kernel,
        out_shape=(jax.ShapeDtypeStruct((R, LZ, K), f32), halo, halo, jax.ShapeDtypeStruct((R, K), bf16)),
        in_specs=[whole(pltpu.SMEM), whole(pltpu.HBM), whole(pltpu.HBM), whole(pl.ANY)],
        out_specs=(whole(),) * 4,
        scratch_shapes=[
            VMEM((D, R * LZ, K), bf16),
            VMEM((D, K, K), bf16),
            pltpu.SemaphoreType.DMA((D,)),
            pltpu.SemaphoreType.DMA((D,)),
        ],
        compiler_params=params(50),
        cost_estimate=pl.CostEstimate(flops=6 * 10**9, bytes_accessed=23 * 10**6, transcendentals=0),
    )(core, x, h, behind)


def wave_kernel(x_ref, coef_ref, panel_ref, behind_ref, out_ref):
    chunks = [x_ref[i].astype(f32)[8:] for i in range(D)]
    profile = jnp.concatenate([x[:, k * NY : k * NY + LZ] for x in chunks for k in range(2)], axis=0)
    panel = panel_ref[...]
    for r in range(R):
        weights = profile * coef_ref[:, r : r + 1]
        log = jnp.zeros((LZ, 256), f32)
        for _ in range(3):
            term = weights.astype(bf16)
            weights = weights - term.astype(f32)
            log = log + lax.dot_general(term, panel, (((0,), (0,)), ((), ())), preferred_element_type=f32)
        out_ref[r] = WAVE_SCALE * jnp.exp(-2.0 * log)


def wave(x, coef, panel, behind):
    return pl.pallas_call(
        wave_kernel,
        out_shape=jax.ShapeDtypeStruct((R, LZ, 256), f32),
        in_specs=[whole()] * 3 + [whole(pl.ANY)],
        out_specs=whole(),
        compiler_params=params(8),
        cost_estimate=pl.CostEstimate(flops=3 * 10**8, bytes_accessed=2 * 10**6, transcendentals=2 * 10**5),
    )(x, coef, panel, behind)


def residual_kernel(core_ref, y_ref, rhs_ref, inner_ref, outer_ref, prev_ref, v_ref, nl_ref, vi_ref, vo_ref, wave_ref, sol_ref, res_ref):
    odd = core_ref[0] > 0
    row = lax.broadcasted_iota(jnp.int32, (LZ, NY), 0)
    lane = lax.broadcasted_iota(jnp.int32, (LZ, NY), 1)
    for r in range(R):
        s = {}
        for a in range(2):
            for x in range(2):
                cols = slice(a * 256 + x * NY, a * 256 + (x + 1) * NY)
                s[a, x] = jnp.where(row == 0, v_ref[r : r + 1, cols], y_ref[r, :, cols])
        lap = {}
        for a in range(2):
            ends = slice(a * NY, (a + 1) * NY)
            inner = jnp.where(row == 0, vi_ref[r : r + 1, ends].astype(f32), inner_ref[r, a].astype(f32))
            outer = jnp.where(row == 0, vo_ref[r : r + 1, ends].astype(f32), outer_ref[r, a].astype(f32))
            below, above = jnp.where(odd, inner, outer), jnp.where(odd, outer, inner)
            for x in range(2):
                cols = slice(a * 256 + x * NY, a * 256 + (x + 1) * NY)
                own = s[a, x]
                before = jnp.where(row == 0, prev_ref[r : r + 1, cols].astype(f32), pltpu.roll(own, 1, 0))
                after = jnp.where(row == LZ - 1, nl_ref[r : r + 1, cols].astype(f32), pltpu.roll(own, LZ - 1, 0))
                left = jnp.where(lane == 0, 0.0, pltpu.roll(own, 1, 1))
                right = jnp.where(lane == NY - 1, 0.0, pltpu.roll(own, NY - 1, 1))
                beside = before + after + left + right
                beside = beside + (below if x == 0 else s[a, 0]) + (s[a, 1] if x == 0 else above)
                lap[a, x] = 6.0 * own - beside
        for x in range(2):
            w = wave_ref[r, :, x * NY : (x + 1) * NY]
            rows = pl.ds(x, LZ, stride=2)
            real = lap[0, x] - w * s[0, x] + ABSORB_RATE * w * s[1, x]
            imag = lap[1, x] - w * s[1, x] - ABSORB_RATE * w * s[0, x]
            sol_ref[0, r, rows, :] = s[0, x]
            sol_ref[1, r, rows, :] = s[1, x]
            res_ref[0, r, rows, :] = rhs_ref[0, r, rows, :] - real
            res_ref[1, r, rows, :] = rhs_ref[1, r, rows, :] - imag


def residual(*args):
    shape = jax.ShapeDtypeStruct((2, R, 2 * LZ, NY), f32)
    return pl.pallas_call(
        residual_kernel,
        out_shape=(shape, shape),
        in_specs=[whole(pltpu.SMEM)] + [whole()] * (len(args) - 1),
        out_specs=(whole(), whole()),
        compiler_params=params(24),
    )(*args)


def pair_groups(step):
    groups = []
    for k in range(G // 2):
        first = (2 * k + step - 1) % G
        second = (first + 1) % G
        for core in range(2):
            groups.append([g * D + 2 * i + core for g in (first, second) for i in range(C)])
    return groups


def shift(value, axis, by):
    size = lax.axis_size(axis)
    return lax.ppermute(value, axis, [(i, i + by) for i in range(size) if 0 <= i + by < size])


def shards(rhs, inverse_blocks, mode_panel, mode_profile, generator, lattice_index, shift_index):
    group = lax.axis_index("layer")
    flat = rhs.reshape(2, R, 2 * LZ, NY)
    own, chunk = prepare(flat, mode_profile)
    along_x = [[z * 4 + x * 2 + c for x in range(2)] for z in range(4) for c in range(2)]
    along_z = [[z * 4 + x * 2 + c for z in range(4) for c in range(2)] for x in range(2)]
    paired = lax.all_gather(own, "plane", axis=0, axis_index_groups=along_x)
    heads = lax.all_to_all(chunk, "plane", 0, 0)
    blocks, _ = lax.optimization_barrier((inverse_blocks, chunk))
    h = arrange(blocks.reshape(K, 2, 32, NY))
    heads, _ = lax.optimization_barrier((heads, h))

    mixed = (lattice_index[None, :] * generator[:, None] + shift_index.T) % NPTS
    amplitude = 0.25 / jnp.sqrt(1.0 + jnp.arange(MODES, dtype=f32) / 8.0)
    coef = amplitude[:, None] * ((mixed.astype(f32) + 0.5) / NPTS - 0.5)
    core = lax.rem(lax.axis_index("plane"), 2).astype(jnp.int32).reshape(1)
    twin = [(i, i ^ 1) for i in range(D)]
    next_chip = [(i, i + 1) for i in range(1, D - 1, 2)] + [(i + 1, i) for i in range(1, D - 1, 2)]

    base, out, keep = first_product(core, h, heads)
    v = base
    for step in range(1, G):
        if step == 2:
            paired, _ = lax.optimization_barrier((paired, v))
            gathered = lax.all_gather(paired, "plane", axis=0, axis_index_groups=along_z).reshape(D, R * LZ, K)
        got = lax.all_to_all(out, ("layer", "plane"), 0, 0, axis_index_groups=pair_groups(step))
        if step == 2:
            wavenum = wave(heads, coef, mode_panel.reshape(MODES, 256), v)
            got, wavenum = lax.optimization_barrier((got, wavenum))
        if step == 6:
            y, inner, outer, last = fronts_of(core, gathered, h, v)
            got, inner, outer, last = lax.optimization_barrier((got, inner, outer, last))
        if step == 7:
            inner, outer, last, v = lax.optimization_barrier((inner, outer, last, v))
            outer = lax.ppermute(outer, "plane", next_chip)
            inner = lax.ppermute(inner, "plane", twin)
            last = shift(last, "layer", 1)
            got, inner, outer, last = lax.optimization_barrier((got, inner, outer, last))
        other = lax.ppermute(got, "plane", twin)
        half = own_half(core, h, keep, got)
        mine = (group == step).astype(jnp.int32).reshape(1)
        v, out, *ends = other_half(core, mine, h, other, half, base, v, step == G - 1)

    v_outer = lax.ppermute(ends[0][0], "plane", next_chip)
    v_next = shift(out, "layer", -1)
    v_inner = lax.ppermute(ends[0][1], "plane", twin)
    sol, res = residual(core, y, flat, inner, outer, last, v, v_next, v_inner, v_outer, wavenum)
    return sol.reshape(rhs.shape), res.reshape(rhs.shape)


def solution(mesh):
    return jax.shard_map(
        shards,
        mesh=mesh,
        in_specs=(
            P(None, None, "layer", "plane", None),
            P("layer", None, "plane", None, None, None, None),
            P(None, "plane", None),
            P("plane", "layer"),
            P(),
            P(),
            P(),
        ),
        out_specs=(P(None, None, "layer", "plane", None), P(None, None, "layer", "plane", None)),
        check_vma=False,
    )
```

```python
import jax
import jax.numpy as jnp
from jax import lax
from jax.experimental import pallas as pl
from jax.experimental.pallas import tpu as pltpu
from jax.sharding import PartitionSpec as P

MODES = 256
NPTS = 32768
COUPLING = 0.8
ABSORB_RATE = 0.3
WAVE_SCALE = 0.8

G = 8
D = 16
C = 8
LZ = 96
R = 8
K = 512
NY = 128
KEEP = 4

bf16 = jnp.bfloat16
f32 = jnp.float32
VMEM = pltpu.VMEM


def whole(space=VMEM):
    return pl.BlockSpec(memory_space=space)


def params(mib):
    return pltpu.CompilerParams(vmem_limit_bytes=mib * 2**20)


def dot_t(x, h):
    return lax.dot_general(x, h, (((1,), (1,)), ((), ())), preferred_element_type=f32)


def prepare_kernel(rhs_ref, profile_ref, x_ref, chunk_ref):
    for a in range(2):
        for x in range(2):
            cols = pl.ds(a * 256 + x * NY, NY)
            for r in range(R):
                x_ref[pl.ds(r * LZ, LZ), cols] = rhs_ref[a, r, pl.ds(x, LZ, stride=2), :].astype(bf16)
    head = jnp.concatenate([rhs_ref[a, :, x, :] for a in range(2) for x in range(2)], axis=1)
    profile = profile_ref[...].astype(f32)
    gap = jnp.zeros((8, NY - LZ), f32)
    tail = jnp.concatenate([profile[:8], gap, profile[8:], gap, jnp.zeros((8, K - 2 * NY), f32)], axis=1)
    chunk = jnp.concatenate([head, tail], axis=0).astype(bf16)
    for i in range(D):
        chunk_ref[i] = chunk


def prepare(rhs, profile):
    return pl.pallas_call(
        prepare_kernel,
        out_shape=(jax.ShapeDtypeStruct((R * LZ, K), bf16), jax.ShapeDtypeStruct((D, 16, K), bf16)),
        in_specs=[whole(), whole()],
        out_specs=(whole(), whole()),
        compiler_params=params(8),
    )(rhs, profile)


def arrange_kernel(blocks_ref, h_ref, in_buf, out_buf, in_sem, out_sem):
    m = lax.broadcasted_iota(jnp.int32, (256, 256), 0)
    n = lax.broadcasted_iota(jnp.int32, (256, 256), 1)
    swap = ((m // 16 == n % 16) & (m % 16 == n // 16)).astype(f32).astype(bf16)

    def rows(i):
        return pl.ds(pl.multiple_of(i * 32, 32), 32)

    def load(i):
        return pltpu.make_async_copy(blocks_ref.at[rows(i)], in_buf.at[i], in_sem.at[i])

    def store(i):
        return pltpu.make_async_copy(out_buf.at[:, :, rows(i)], h_ref.at[:, :, rows(i)], out_sem.at[i])

    for i in range(K // 32):
        load(i).start()

    @pl.loop(0, K // 32)
    def _(i):
        load(i).wait()
        for s in range(2):
            for half in range(2):
                tile = jnp.concatenate(
                    [in_buf[i, pl.ds(s * 16, 16), c, pl.ds(half * 16, 16), :].reshape(256, NY) for c in range(2)], axis=1
                )
                moved = jnp.dot(swap, tile, preferred_element_type=f32).astype(bf16)
                for q in range(16):
                    p = half * 16 + q
                    source = p // 2
                    into = pl.ds(pl.multiple_of(i * 32 + s * 16, 16), 16)
                    for c in range(2):
                        out_buf[source % 2, source // 2, into, pl.ds(c * 256 + (p % 2) * NY, NY)] = moved[
                            q * 16 : (q + 1) * 16, c * NY : (c + 1) * NY
                        ]
        store(i).start()

    for i in range(K // 32):
        store(i).wait()


def arrange(blocks):
    return pl.pallas_call(
        arrange_kernel,
        out_shape=jax.ShapeDtypeStruct((2, C, K, K), bf16),
        in_specs=[whole(pltpu.HBM)],
        out_specs=whole(pltpu.HBM),
        scratch_shapes=[
            VMEM((K // 32, 32, 2, 32, NY), bf16),
            VMEM((2, C, K, K), bf16),
            pltpu.SemaphoreType.DMA((K // 32,)),
            pltpu.SemaphoreType.DMA((K // 32,)),
        ],
        compiler_params=params(50),
        cost_estimate=pl.CostEstimate(flops=4 * 10**9, bytes_accessed=17 * 10**6, transcendentals=0),
    )(blocks)


COST = pl.CostEstimate(flops=10**8, bytes_accessed=5 * 10**6, transcendentals=0)


def fetch(h_ref, buf, sem, core, first=0):
    copies = [pltpu.make_async_copy(h_ref.at[core, k], buf.at[k], sem.at[k]) for k in range(first, C)]
    for copy in copies:
        copy.start()
    return copies


def first_kernel(core_ref, h_ref, x_ref, v_ref, out_ref, keep_ref, even, odd, even_sem, odd_sem):
    bufs = (even, odd)
    copies = [fetch(h_ref, bufs[core], (even_sem, odd_sem)[core], core) for core in range(2)]
    acc = jnp.zeros((16, K), f32)
    for core in range(2):
        for k in range(C):
            copies[core][k].wait()
            acc = acc + dot_t(x_ref[2 * k + core], bufs[core][k])
    v = acc[:R]
    v_ref[...] = v
    for i in range(D):
        out_ref[i] = v.astype(bf16)
    for core in range(2):

        @pl.when(core_ref[0] == core)
        def _():
            for k in range(KEEP):
                keep_ref[k] = bufs[core][k]


HALF = [VMEM((C, K, K), bf16)]
SEMS = [pltpu.SemaphoreType.DMA((C,))]


def first_product(core, h, x):
    return pl.pallas_call(
        first_kernel,
        out_shape=MATVEC_OUT + (jax.ShapeDtypeStruct((KEEP, K, K), bf16),),
        in_specs=[whole(pltpu.SMEM), whole(pltpu.HBM), whole()],
        out_specs=(whole(),) * 3,
        scratch_shapes=HALF * 2 + SEMS * 2,
        compiler_params=params(50),
        cost_estimate=COST,
    )(core, h, x)


def own_kernel(core_ref, h_ref, keep_ref, x_ref, acc_ref, buf, sem):
    copies = fetch(h_ref, buf, sem, core_ref[0], KEEP)
    acc = jnp.zeros((R, K), f32)
    for k in range(KEEP):
        acc = acc + dot_t(x_ref[k], keep_ref[k])
    for k in range(KEEP, C):
        copies[k - KEEP].wait()
        acc = acc + dot_t(x_ref[k], buf[k])
    acc_ref[...] = acc


def own_half(core, h, keep, x):
    return pl.pallas_call(
        own_kernel,
        out_shape=jax.ShapeDtypeStruct((R, K), f32),
        in_specs=[whole(pltpu.SMEM), whole(pltpu.HBM), whole(), whole()],
        out_specs=whole(),
        scratch_shapes=HALF + SEMS,
        compiler_params=params(50),
        cost_estimate=COST,
    )(core, h, keep, x)


def other_kernel(core_ref, mine_ref, h_ref, x_ref, half_ref, base_ref, old_ref, v_ref, out_ref, buf, sem, ends_ref=None):
    acc = half_ref[...]
    for k, copy in enumerate(fetch(h_ref, buf, sem, 1 - core_ref[0])):
        copy.wait()
        acc = acc + dot_t(x_ref[k], buf[k])
    v = jnp.where(mine_ref[0] > 0, base_ref[...] + COUPLING * acc, old_ref[...])
    v_ref[...] = v
    rounded = v.astype(bf16)
    if ends_ref is None:
        for i in range(D):
            out_ref[i] = rounded
        return
    out_ref[...] = rounded
    low = jnp.concatenate([rounded[:, :NY], rounded[:, 2 * NY : 3 * NY]], axis=1)
    high = jnp.concatenate([rounded[:, NY : 2 * NY], rounded[:, 3 * NY :]], axis=1)
    odd = core_ref[0] > 0
    ends_ref[0] = jnp.where(odd, high, low)
    ends_ref[1] = jnp.where(odd, low, high)


def final_kernel(core_ref, mine_ref, h_ref, x_ref, half_ref, base_ref, old_ref, v_ref, out_ref, ends_ref, buf, sem):
    other_kernel(core_ref, mine_ref, h_ref, x_ref, half_ref, base_ref, old_ref, v_ref, out_ref, buf, sem, ends_ref)


MATVEC_OUT = (jax.ShapeDtypeStruct((R, K), f32), jax.ShapeDtypeStruct((D, R, K), bf16))


def other_half(core, mine, h, x, half, base, old, final):
    out = MATVEC_OUT
    if final:
        out = (out[0], jax.ShapeDtypeStruct((R, K), bf16), jax.ShapeDtypeStruct((2, R, 256), bf16))
    return pl.pallas_call(
        final_kernel if final else other_kernel,
        out_shape=out,
        in_specs=[whole(pltpu.SMEM)] * 2 + [whole(pltpu.HBM)] + [whole()] * 4,
        out_specs=(whole(),) * len(out),
        scratch_shapes=HALF + SEMS,
        compiler_params=params(50),
        cost_estimate=COST,
    )(core, mine, h, x, half, base, old)


def fronts_kernel(
    core_ref, x_ref, h_ref, behind_ref, y_out, inner_out, outer_out, last_ref, y_ref, inner_ref, outer_ref, x_buf, h_buf, x_sem, h_sem, out_sem
):
    def loads(i):
        core, chip = lax.rem(lax.div(i, 2), 2), lax.div(i, 4) * 2 + lax.rem(i, 2)
        return (
            pltpu.make_async_copy(x_ref.at[i], x_buf.at[i], x_sem.at[i]),
            pltpu.make_async_copy(h_ref.at[core, chip], h_buf.at[i], h_sem.at[i]),
        )

    @pl.loop(0, D)
    def _(i):
        for copy in loads(i):
            copy.start()

    y_ref[...] = jnp.zeros((R, LZ, K), f32)

    @pl.loop(0, D // 2)
    def _(j):
        for i in (2 * j, 2 * j + 1):
            for copy in loads(i):
                copy.wait()
        total = dot_t(x_buf[2 * j], h_buf[2 * j]) + dot_t(x_buf[2 * j + 1], h_buf[2 * j + 1])
        y_ref[...] += total.reshape(R, LZ, K)

    stores = [
        pltpu.make_async_copy(y_ref, y_out, out_sem.at[0]),
        pltpu.make_async_copy(inner_ref, inner_out, out_sem.at[1]),
        pltpu.make_async_copy(outer_ref, outer_out, out_sem.at[2]),
    ]
    stores[0].start()
    odd = core_ref[0] > 0
    for r in range(R):
        for a in range(2):
            low = y_ref[r, :, a * 256 : a * 256 + NY].astype(bf16)
            high = y_ref[r, :, a * 256 + NY : a * 256 + 256].astype(bf16)
            inner_ref[r, a] = jnp.where(odd, low, high)
            outer_ref[r, a] = jnp.where(odd, high, low)
    for store in stores[1:]:
        store.start()
    last_ref[...] = jnp.concatenate([y_ref[r, LZ - 1 : LZ, :] for r in range(R)], axis=0).astype(bf16)
    for store in stores:
        store.wait()


def fronts_of(core, x, h, behind):
    halo = jax.ShapeDtypeStruct((R, 2, LZ, NY), bf16)
    return pl.pallas_call(
        fronts_kernel,
        out_shape=(jax.ShapeDtypeStruct((R, LZ, K), f32), halo, halo, jax.ShapeDtypeStruct((R, K), bf16)),
        in_specs=[whole(pltpu.SMEM), whole(pltpu.HBM), whole(pltpu.HBM), whole(pl.ANY)],
        out_specs=(whole(pltpu.HBM),) * 3 + (whole(),),
        scratch_shapes=[
            VMEM((R, LZ, K), f32),
            VMEM((R, 2, LZ, NY), bf16),
            VMEM((R, 2, LZ, NY), bf16),
            VMEM((D, R * LZ, K), bf16),
            VMEM((D, K, K), bf16),
            pltpu.SemaphoreType.DMA((D,)),
            pltpu.SemaphoreType.DMA((D,)),
            pltpu.SemaphoreType.DMA((3,)),
        ],
        compiler_params=params(52),
        cost_estimate=pl.CostEstimate(flops=6 * 10**9, bytes_accessed=23 * 10**6, transcendentals=0),
    )(core, x, h, behind)


def wave_kernel(x_ref, coef_ref, panel_ref, behind_ref, out_ref):
    chunks = [x_ref[i].astype(f32)[8:] for i in range(D)]
    profile = jnp.concatenate([x[:, k * NY : k * NY + LZ] for x in chunks for k in range(2)], axis=0)
    panel = panel_ref[...]
    for r in range(R):
        weights = profile * coef_ref[:, r : r + 1]
        log = jnp.zeros((LZ, 256), f32)
        for _ in range(3):
            term = weights.astype(bf16)
            weights = weights - term.astype(f32)
            log = log + lax.dot_general(term, panel, (((0,), (0,)), ((), ())), preferred_element_type=f32)
        out_ref[r] = WAVE_SCALE * jnp.exp(-2.0 * log)


def wave(x, coef, panel, behind):
    return pl.pallas_call(
        wave_kernel,
        out_shape=jax.ShapeDtypeStruct((R, LZ, 256), f32),
        in_specs=[whole()] * 3 + [whole(pl.ANY)],
        out_specs=whole(),
        compiler_params=params(8),
        cost_estimate=pl.CostEstimate(flops=3 * 10**8, bytes_accessed=2 * 10**6, transcendentals=2 * 10**5),
    )(x, coef, panel, behind)


def residual_kernel(core_ref, y_ref, rhs_ref, inner_ref, outer_ref, prev_ref, v_ref, nl_ref, vi_ref, vo_ref, wave_ref, sol_ref, res_ref):
    odd = core_ref[0] > 0
    row = lax.broadcasted_iota(jnp.int32, (LZ, NY), 0)
    lane = lax.broadcasted_iota(jnp.int32, (LZ, NY), 1)
    for r in range(R):
        s = {}
        for a in range(2):
            for x in range(2):
                cols = slice(a * 256 + x * NY, a * 256 + (x + 1) * NY)
                s[a, x] = jnp.where(row == 0, v_ref[r : r + 1, cols], y_ref[r, :, cols])
        lap = {}
        for a in range(2):
            ends = slice(a * NY, (a + 1) * NY)
            inner = jnp.where(row == 0, vi_ref[r : r + 1, ends].astype(f32), inner_ref[r, a].astype(f32))
            outer = jnp.where(row == 0, vo_ref[r : r + 1, ends].astype(f32), outer_ref[r, a].astype(f32))
            below, above = jnp.where(odd, inner, outer), jnp.where(odd, outer, inner)
            for x in range(2):
                cols = slice(a * 256 + x * NY, a * 256 + (x + 1) * NY)
                own = s[a, x]
                before = jnp.where(row == 0, prev_ref[r : r + 1, cols].astype(f32), pltpu.roll(own, 1, 0))
                after = jnp.where(row == LZ - 1, nl_ref[r : r + 1, cols].astype(f32), pltpu.roll(own, LZ - 1, 0))
                left = jnp.where(lane == 0, 0.0, pltpu.roll(own, 1, 1))
                right = jnp.where(lane == NY - 1, 0.0, pltpu.roll(own, NY - 1, 1))
                beside = before + after + left + right
                beside = beside + (below if x == 0 else s[a, 0]) + (s[a, 1] if x == 0 else above)
                lap[a, x] = 6.0 * own - beside
        for x in range(2):
            w = wave_ref[r, :, x * NY : (x + 1) * NY]
            rows = pl.ds(x, LZ, stride=2)
            real = lap[0, x] - w * s[0, x] + ABSORB_RATE * w * s[1, x]
            imag = lap[1, x] - w * s[1, x] - ABSORB_RATE * w * s[0, x]
            sol_ref[0, r, rows, :] = s[0, x]
            sol_ref[1, r, rows, :] = s[1, x]
            res_ref[0, r, rows, :] = rhs_ref[0, r, rows, :] - real
            res_ref[1, r, rows, :] = rhs_ref[1, r, rows, :] - imag


def residual(*args):
    shape = jax.ShapeDtypeStruct((2, R, 2 * LZ, NY), f32)
    return pl.pallas_call(
        residual_kernel,
        out_shape=(shape, shape),
        in_specs=[whole(pltpu.SMEM)] + [whole()] * (len(args) - 1),
        out_specs=(whole(), whole()),
        compiler_params=params(24),
    )(*args)


def pair_groups(step):
    groups = []
    for k in range(G // 2):
        first = (2 * k + step - 1) % G
        second = (first + 1) % G
        for core in range(2):
            groups.append([g * D + 2 * i + core for g in (first, second) for i in range(C)])
    return groups


def shift(value, axis, by):
    size = lax.axis_size(axis)
    return lax.ppermute(value, axis, [(i, i + by) for i in range(size) if 0 <= i + by < size])


def shards(rhs, inverse_blocks, mode_panel, mode_profile, generator, lattice_index, shift_index):
    group = lax.axis_index("layer")
    flat = rhs.reshape(2, R, 2 * LZ, NY)
    own, chunk = prepare(flat, mode_profile)
    along_x = [[z * 4 + x * 2 + c for x in range(2)] for z in range(4) for c in range(2)]
    along_z = [[z * 4 + x * 2 + c for z in range(4) for c in range(2)] for x in range(2)]
    paired = lax.all_gather(own, "plane", axis=0, axis_index_groups=along_x)
    heads = lax.all_to_all(chunk, "plane", 0, 0)
    blocks, _ = lax.optimization_barrier((inverse_blocks, chunk))
    h = arrange(blocks.reshape(K, 2, 32, NY))
    heads, _ = lax.optimization_barrier((heads, h))

    mixed = (lattice_index[None, :] * generator[:, None] + shift_index.T) % NPTS
    amplitude = 0.25 / jnp.sqrt(1.0 + jnp.arange(MODES, dtype=f32) / 8.0)
    coef = amplitude[:, None] * ((mixed.astype(f32) + 0.5) / NPTS - 0.5)
    core = lax.rem(lax.axis_index("plane"), 2).astype(jnp.int32).reshape(1)
    twin = [(i, i ^ 1) for i in range(D)]
    next_chip = [(i, i + 1) for i in range(1, D - 1, 2)] + [(i + 1, i) for i in range(1, D - 1, 2)]

    base, out, keep = first_product(core, h, heads)
    v = base
    for step in range(1, G):
        if step == 2:
            paired, _ = lax.optimization_barrier((paired, v))
            gathered = lax.all_gather(paired, "plane", axis=0, axis_index_groups=along_z).reshape(D, R * LZ, K)
        got = lax.all_to_all(out, ("layer", "plane"), 0, 0, axis_index_groups=pair_groups(step))
        if step == 2:
            wavenum = wave(heads, coef, mode_panel.reshape(MODES, 256), v)
            got, wavenum = lax.optimization_barrier((got, wavenum))
        if step == 6:
            y, inner, outer, last = fronts_of(core, gathered, h, v)
            got, inner, outer, last = lax.optimization_barrier((got, inner, outer, last))
        if step == 7:
            last, v = lax.optimization_barrier((last, v))
            last = shift(last, "layer", 1)
            got, inner, outer, last = lax.optimization_barrier((got, inner, outer, last))
            outer = lax.ppermute(outer, "plane", next_chip)
            inner = lax.ppermute(inner, "plane", twin)
        other = lax.ppermute(got, "plane", twin)
        half = own_half(core, h, keep, got)
        mine = (group == step).astype(jnp.int32).reshape(1)
        v, out, *ends = other_half(core, mine, h, other, half, base, v, step == G - 1)

    v_outer = lax.ppermute(ends[0][0], "plane", next_chip)
    v_next = shift(out, "layer", -1)
    v_inner = lax.ppermute(ends[0][1], "plane", twin)
    sol, res = residual(core, y, flat, inner, outer, last, v, v_next, v_inner, v_outer, wavenum)
    return sol.reshape(rhs.shape), res.reshape(rhs.shape)


def solution(mesh):
    return jax.shard_map(
        shards,
        mesh=mesh,
        in_specs=(
            P(None, None, "layer", "plane", None),
            P("layer", None, "plane", None, None, None, None),
            P(None, "plane", None),
            P("plane", "layer"),
            P(),
            P(),
            P(),
        ),
        out_specs=(P(None, None, "layer", "plane", None), P(None, None, "layer", "plane", None)),
        check_vma=False,
    )
```

```python
import jax
import jax.numpy as jnp
from jax import lax
from jax.experimental import pallas as pl
from jax.experimental.pallas import tpu as pltpu
from jax.sharding import PartitionSpec as P

MODES = 256
NPTS = 32768
COUPLING = 0.8
ABSORB_RATE = 0.3
WAVE_SCALE = 0.8

G = 8
D = 16
C = 8
LZ = 96
R = 8
K = 512
NY = 128
KEEP = 3

bf16 = jnp.bfloat16
f32 = jnp.float32
VMEM = pltpu.VMEM


def whole(space=VMEM):
    return pl.BlockSpec(memory_space=space)


def params(mib):
    return pltpu.CompilerParams(vmem_limit_bytes=mib * 2**20)


def dot_t(x, h):
    return lax.dot_general(x, h, (((1,), (1,)), ((), ())), preferred_element_type=f32)


def prepare_kernel(rhs_ref, profile_ref, x_ref, chunk_ref):
    for a in range(2):
        for x in range(2):
            cols = pl.ds(a * 256 + x * NY, NY)
            for r in range(R):
                x_ref[pl.ds(r * LZ, LZ), cols] = rhs_ref[a, r, pl.ds(x, LZ, stride=2), :].astype(bf16)
    head = jnp.concatenate([rhs_ref[a, :, x, :] for a in range(2) for x in range(2)], axis=1)
    profile = profile_ref[...].astype(f32)
    gap = jnp.zeros((8, NY - LZ), f32)
    tail = jnp.concatenate([profile[:8], gap, profile[8:], gap, jnp.zeros((8, K - 2 * NY), f32)], axis=1)
    chunk = jnp.concatenate([head, tail], axis=0).astype(bf16)
    for i in range(D):
        chunk_ref[i] = chunk


def prepare(rhs, profile):
    return pl.pallas_call(
        prepare_kernel,
        out_shape=(jax.ShapeDtypeStruct((R * LZ, K), bf16), jax.ShapeDtypeStruct((D, 16, K), bf16)),
        in_specs=[whole(), whole()],
        out_specs=(whole(), whole()),
        compiler_params=params(8),
    )(rhs, profile)


def arrange_kernel(blocks_ref, h_ref, in_buf, out_buf, in_sem, out_sem):
    m = lax.broadcasted_iota(jnp.int32, (256, 256), 0)
    n = lax.broadcasted_iota(jnp.int32, (256, 256), 1)
    swap = ((m // 16 == n % 16) & (m % 16 == n // 16)).astype(f32).astype(bf16)

    def rows(i):
        return pl.ds(pl.multiple_of(i * 32, 32), 32)

    def load(i):
        return pltpu.make_async_copy(blocks_ref.at[rows(i)], in_buf.at[i], in_sem.at[i])

    def store(i):
        return pltpu.make_async_copy(out_buf.at[:, :, rows(i)], h_ref.at[:, :, rows(i)], out_sem.at[i])

    for i in range(K // 32):
        load(i).start()

    @pl.loop(0, K // 32)
    def _(i):
        load(i).wait()
        for s in range(2):
            for half in range(2):
                tile = jnp.concatenate(
                    [in_buf[i, pl.ds(s * 16, 16), c, pl.ds(half * 16, 16), :].reshape(256, NY) for c in range(2)], axis=1
                )
                moved = jnp.dot(swap, tile, preferred_element_type=f32).astype(bf16)
                for q in range(16):
                    p = half * 16 + q
                    source = p // 2
                    into = pl.ds(pl.multiple_of(i * 32 + s * 16, 16), 16)
                    for c in range(2):
                        out_buf[source % 2, source // 2, into, pl.ds(c * 256 + (p % 2) * NY, NY)] = moved[
                            q * 16 : (q + 1) * 16, c * NY : (c + 1) * NY
                        ]
        store(i).start()

    for i in range(K // 32):
        store(i).wait()


def arrange(blocks):
    return pl.pallas_call(
        arrange_kernel,
        out_shape=jax.ShapeDtypeStruct((2, C, K, K), bf16),
        in_specs=[whole(pltpu.HBM)],
        out_specs=whole(pltpu.HBM),
        scratch_shapes=[
            VMEM((K // 32, 32, 2, 32, NY), bf16),
            VMEM((2, C, K, K), bf16),
            pltpu.SemaphoreType.DMA((K // 32,)),
            pltpu.SemaphoreType.DMA((K // 32,)),
        ],
        compiler_params=params(50),
        cost_estimate=pl.CostEstimate(flops=4 * 10**9, bytes_accessed=17 * 10**6, transcendentals=0),
    )(blocks)


COST = pl.CostEstimate(flops=10**8, bytes_accessed=5 * 10**6, transcendentals=0)


def fetch(h_ref, buf, sem, core, first=0):
    copies = [pltpu.make_async_copy(h_ref.at[core, k], buf.at[k], sem.at[k]) for k in range(first, C)]
    for copy in copies:
        copy.start()
    return copies


def first_kernel(core_ref, h_ref, x_ref, v_ref, out_ref, keep_ref, even, odd, even_sem, odd_sem):
    bufs = (even, odd)
    copies = [fetch(h_ref, bufs[core], (even_sem, odd_sem)[core], core) for core in range(2)]
    acc = jnp.zeros((16, K), f32)
    for core in range(2):
        for k in range(C):
            copies[core][k].wait()
            acc = acc + dot_t(x_ref[2 * k + core], bufs[core][k])
    v = acc[:R]
    v_ref[...] = v
    for i in range(D):
        out_ref[i] = v.astype(bf16)
    for core in range(2):

        @pl.when(core_ref[0] == core)
        def _():
            for k in range(KEEP):
                keep_ref[k] = bufs[core][k]


HALF = [VMEM((C, K, K), bf16)]
SEMS = [pltpu.SemaphoreType.DMA((C,))]


def first_product(core, h, x):
    return pl.pallas_call(
        first_kernel,
        out_shape=MATVEC_OUT + (jax.ShapeDtypeStruct((KEEP, K, K), bf16),),
        in_specs=[whole(pltpu.SMEM), whole(pltpu.HBM), whole()],
        out_specs=(whole(),) * 3,
        scratch_shapes=HALF * 2 + SEMS * 2,
        compiler_params=params(50),
        cost_estimate=COST,
    )(core, h, x)


def own_kernel(core_ref, h_ref, keep_ref, x_ref, acc_ref, buf, sem):
    copies = fetch(h_ref, buf, sem, core_ref[0], KEEP)
    acc = jnp.zeros((R, K), f32)
    for k in range(KEEP):
        acc = acc + dot_t(x_ref[k], keep_ref[k])
    for k in range(KEEP, C):
        copies[k - KEEP].wait()
        acc = acc + dot_t(x_ref[k], buf[k])
    acc_ref[...] = acc


def own_half(core, h, keep, x):
    return pl.pallas_call(
        own_kernel,
        out_shape=jax.ShapeDtypeStruct((R, K), f32),
        in_specs=[whole(pltpu.SMEM), whole(pltpu.HBM), whole(), whole()],
        out_specs=whole(),
        scratch_shapes=HALF + SEMS,
        compiler_params=params(50),
        cost_estimate=COST,
    )(core, h, keep, x)


def other_kernel(core_ref, mine_ref, h_ref, x_ref, half_ref, base_ref, old_ref, v_ref, out_ref, buf, sem, ends_ref=None):
    acc = half_ref[...]
    for k, copy in enumerate(fetch(h_ref, buf, sem, 1 - core_ref[0])):
        copy.wait()
        acc = acc + dot_t(x_ref[k], buf[k])
    v = jnp.where(mine_ref[0] > 0, base_ref[...] + COUPLING * acc, old_ref[...])
    v_ref[...] = v
    rounded = v.astype(bf16)
    if ends_ref is None:
        for i in range(D):
            out_ref[i] = rounded
        return
    out_ref[...] = rounded
    low = jnp.concatenate([rounded[:, :NY], rounded[:, 2 * NY : 3 * NY]], axis=1)
    high = jnp.concatenate([rounded[:, NY : 2 * NY], rounded[:, 3 * NY :]], axis=1)
    odd = core_ref[0] > 0
    ends_ref[0] = jnp.where(odd, high, low)
    ends_ref[1] = jnp.where(odd, low, high)


def final_kernel(core_ref, mine_ref, h_ref, x_ref, half_ref, base_ref, old_ref, v_ref, out_ref, ends_ref, buf, sem):
    other_kernel(core_ref, mine_ref, h_ref, x_ref, half_ref, base_ref, old_ref, v_ref, out_ref, buf, sem, ends_ref)


MATVEC_OUT = (jax.ShapeDtypeStruct((R, K), f32), jax.ShapeDtypeStruct((D, R, K), bf16))


def other_half(core, mine, h, x, half, base, old, final):
    out = MATVEC_OUT
    if final:
        out = (out[0], jax.ShapeDtypeStruct((R, K), bf16), jax.ShapeDtypeStruct((2, R, 256), bf16))
    return pl.pallas_call(
        final_kernel if final else other_kernel,
        out_shape=out,
        in_specs=[whole(pltpu.SMEM)] * 2 + [whole(pltpu.HBM)] + [whole()] * 4,
        out_specs=(whole(),) * len(out),
        scratch_shapes=HALF + SEMS,
        compiler_params=params(50),
        cost_estimate=COST,
    )(core, mine, h, x, half, base, old)


def fronts_kernel(core_ref, x_ref, h_ref, behind_ref, y_ref, inner_ref, outer_ref, last_ref, x_buf, h_buf, x_sem, h_sem):
    def loads(i):
        core, chip = lax.rem(lax.div(i, 2), 2), lax.div(i, 4) * 2 + lax.rem(i, 2)
        return (
            pltpu.make_async_copy(x_ref.at[i], x_buf.at[i], x_sem.at[i]),
            pltpu.make_async_copy(h_ref.at[core, chip], h_buf.at[i], h_sem.at[i]),
        )

    @pl.loop(0, D)
    def _(i):
        for copy in loads(i):
            copy.start()

    y_ref[...] = jnp.zeros((R, LZ, K), f32)

    @pl.loop(0, D // 2)
    def _(j):
        for i in (2 * j, 2 * j + 1):
            for copy in loads(i):
                copy.wait()
        total = dot_t(x_buf[2 * j], h_buf[2 * j]) + dot_t(x_buf[2 * j + 1], h_buf[2 * j + 1])
        y_ref[...] += total.reshape(R, LZ, K)

    odd = core_ref[0] > 0
    for r in range(R):
        for a in range(2):
            low = y_ref[r, :, a * 256 : a * 256 + NY].astype(bf16)
            high = y_ref[r, :, a * 256 + NY : a * 256 + 256].astype(bf16)
            inner_ref[r, a] = jnp.where(odd, low, high)
            outer_ref[r, a] = jnp.where(odd, high, low)
    last_ref[...] = jnp.concatenate([y_ref[r, LZ - 1 : LZ, :] for r in range(R)], axis=0).astype(bf16)


def fronts_of(core, x, h, behind):
    halo = jax.ShapeDtypeStruct((R, 2, LZ, NY), bf16)
    return pl.pallas_call(
        fronts_kernel,
        out_shape=(jax.ShapeDtypeStruct((R, LZ, K), f32), halo, halo, jax.ShapeDtypeStruct((R, K), bf16)),
        in_specs=[whole(pltpu.SMEM), whole(pltpu.HBM), whole(pltpu.HBM), whole(pl.ANY)],
        out_specs=(whole(),) * 4,
        scratch_shapes=[
            VMEM((D, R * LZ, K), bf16),
            VMEM((D, K, K), bf16),
            pltpu.SemaphoreType.DMA((D,)),
            pltpu.SemaphoreType.DMA((D,)),
        ],
        compiler_params=params(50),
        cost_estimate=pl.CostEstimate(flops=6 * 10**9, bytes_accessed=23 * 10**6, transcendentals=0),
    )(core, x, h, behind)


def wave_kernel(x_ref, coef_ref, panel_ref, behind_ref, out_ref):
    chunks = [x_ref[i].astype(f32)[8:] for i in range(D)]
    profile = jnp.concatenate([x[:, k * NY : k * NY + LZ] for x in chunks for k in range(2)], axis=0)
    panel = panel_ref[...]
    for r in range(R):
        weights = profile * coef_ref[:, r : r + 1]
        log = jnp.zeros((LZ, 256), f32)
        for _ in range(3):
            term = weights.astype(bf16)
            weights = weights - term.astype(f32)
            log = log + lax.dot_general(term, panel, (((0,), (0,)), ((), ())), preferred_element_type=f32)
        out_ref[r] = WAVE_SCALE * jnp.exp(-2.0 * log)


def wave(x, coef, panel, behind):
    return pl.pallas_call(
        wave_kernel,
        out_shape=jax.ShapeDtypeStruct((R, LZ, 256), f32),
        in_specs=[whole()] * 3 + [whole(pl.ANY)],
        out_specs=whole(),
        compiler_params=params(8),
        cost_estimate=pl.CostEstimate(flops=3 * 10**8, bytes_accessed=2 * 10**6, transcendentals=2 * 10**5),
    )(x, coef, panel, behind)


def residual_kernel(core_ref, y_ref, rhs_ref, inner_ref, outer_ref, prev_ref, v_ref, nl_ref, vi_ref, vo_ref, wave_ref, sol_ref, res_ref):
    odd = core_ref[0] > 0
    row = lax.broadcasted_iota(jnp.int32, (LZ, NY), 0)
    lane = lax.broadcasted_iota(jnp.int32, (LZ, NY), 1)
    for r in range(R):
        s = {}
        for a in range(2):
            for x in range(2):
                cols = slice(a * 256 + x * NY, a * 256 + (x + 1) * NY)
                s[a, x] = jnp.where(row == 0, v_ref[r : r + 1, cols], y_ref[r, :, cols])
        lap = {}
        for a in range(2):
            ends = slice(a * NY, (a + 1) * NY)
            inner = jnp.where(row == 0, vi_ref[r : r + 1, ends].astype(f32), inner_ref[r, a].astype(f32))
            outer = jnp.where(row == 0, vo_ref[r : r + 1, ends].astype(f32), outer_ref[r, a].astype(f32))
            below, above = jnp.where(odd, inner, outer), jnp.where(odd, outer, inner)
            for x in range(2):
                cols = slice(a * 256 + x * NY, a * 256 + (x + 1) * NY)
                own = s[a, x]
                before = jnp.where(row == 0, prev_ref[r : r + 1, cols].astype(f32), pltpu.roll(own, 1, 0))
                after = jnp.where(row == LZ - 1, nl_ref[r : r + 1, cols].astype(f32), pltpu.roll(own, LZ - 1, 0))
                left = jnp.where(lane == 0, 0.0, pltpu.roll(own, 1, 1))
                right = jnp.where(lane == NY - 1, 0.0, pltpu.roll(own, NY - 1, 1))
                beside = before + after + left + right
                beside = beside + (below if x == 0 else s[a, 0]) + (s[a, 1] if x == 0 else above)
                lap[a, x] = 6.0 * own - beside
        for x in range(2):
            w = wave_ref[r, :, x * NY : (x + 1) * NY]
            rows = pl.ds(x, LZ, stride=2)
            real = lap[0, x] - w * s[0, x] + ABSORB_RATE * w * s[1, x]
            imag = lap[1, x] - w * s[1, x] - ABSORB_RATE * w * s[0, x]
            sol_ref[0, r, rows, :] = s[0, x]
            sol_ref[1, r, rows, :] = s[1, x]
            res_ref[0, r, rows, :] = rhs_ref[0, r, rows, :] - real
            res_ref[1, r, rows, :] = rhs_ref[1, r, rows, :] - imag


def residual(*args):
    shape = jax.ShapeDtypeStruct((2, R, 2 * LZ, NY), f32)
    return pl.pallas_call(
        residual_kernel,
        out_shape=(shape, shape),
        in_specs=[whole(pltpu.SMEM)] + [whole()] * (len(args) - 1),
        out_specs=(whole(), whole()),
        compiler_params=params(24),
    )(*args)


def pair_groups(step):
    groups = []
    for k in range(G // 2):
        first = (2 * k + step - 1) % G
        second = (first + 1) % G
        for core in range(2):
            groups.append([g * D + 2 * i + core for g in (first, second) for i in range(C)])
    return groups


def shift(value, axis, by):
    size = lax.axis_size(axis)
    return lax.ppermute(value, axis, [(i, i + by) for i in range(size) if 0 <= i + by < size])


def shards(rhs, inverse_blocks, mode_panel, mode_profile, generator, lattice_index, shift_index):
    group = lax.axis_index("layer")
    flat = rhs.reshape(2, R, 2 * LZ, NY)
    own, chunk = prepare(flat, mode_profile)
    along_x = [[z * 4 + x * 2 + c for x in range(2)] for z in range(4) for c in range(2)]
    along_z = [[z * 4 + x * 2 + c for z in range(4) for c in range(2)] for x in range(2)]
    paired = lax.all_gather(own, "plane", axis=0, axis_index_groups=along_x)
    heads = lax.all_to_all(chunk, "plane", 0, 0)
    blocks, _ = lax.optimization_barrier((inverse_blocks, chunk))
    h = arrange(blocks.reshape(K, 2, 32, NY))
    heads, _ = lax.optimization_barrier((heads, h))

    mixed = (lattice_index[None, :] * generator[:, None] + shift_index.T) % NPTS
    amplitude = 0.25 / jnp.sqrt(1.0 + jnp.arange(MODES, dtype=f32) / 8.0)
    coef = amplitude[:, None] * ((mixed.astype(f32) + 0.5) / NPTS - 0.5)
    core = lax.rem(lax.axis_index("plane"), 2).astype(jnp.int32).reshape(1)
    twin = [(i, i ^ 1) for i in range(D)]
    next_chip = [(i, i + 1) for i in range(1, D - 1, 2)] + [(i + 1, i) for i in range(1, D - 1, 2)]

    base, out, keep = first_product(core, h, heads)
    v = base
    for step in range(1, G):
        if step == 2:
            paired, _ = lax.optimization_barrier((paired, v))
            gathered = lax.all_gather(paired, "plane", axis=0, axis_index_groups=along_z).reshape(D, R * LZ, K)
        got = lax.all_to_all(out, ("layer", "plane"), 0, 0, axis_index_groups=pair_groups(step))
        if step == 2:
            wavenum = wave(heads, coef, mode_panel.reshape(MODES, 256), v)
            got, wavenum = lax.optimization_barrier((got, wavenum))
        if step == 6:
            y, inner, outer, last = fronts_of(core, gathered, h, v)
            got, inner, outer, last = lax.optimization_barrier((got, inner, outer, last))
        if step == 7:
            last, v = lax.optimization_barrier((last, v))
            last = shift(last, "layer", 1)
            got, inner, outer, last = lax.optimization_barrier((got, inner, outer, last))
            outer = lax.ppermute(outer, "plane", next_chip)
            inner = lax.ppermute(inner, "plane", twin)
        other = lax.ppermute(got, "plane", twin)
        half = own_half(core, h, keep, got)
        mine = (group == step).astype(jnp.int32).reshape(1)
        v, out, *ends = other_half(core, mine, h, other, half, base, v, step == G - 1)

    v_outer = lax.ppermute(ends[0][0], "plane", next_chip)
    v_next = shift(out, "layer", -1)
    v_inner = lax.ppermute(ends[0][1], "plane", twin)
    sol, res = residual(core, y, flat, inner, outer, last, v, v_next, v_inner, v_outer, wavenum)
    return sol.reshape(rhs.shape), res.reshape(rhs.shape)


def solution(mesh):
    return jax.shard_map(
        shards,
        mesh=mesh,
        in_specs=(
            P(None, None, "layer", "plane", None),
            P("layer", None, "plane", None, None, None, None),
            P(None, "plane", None),
            P("plane", "layer"),
            P(),
            P(),
            P(),
        ),
        out_specs=(P(None, None, "layer", "plane", None), P(None, None, "layer", "plane", None)),
        check_vma=False,
    )
```

```python
import jax
import jax.numpy as jnp
from jax import lax
from jax.experimental import pallas as pl
from jax.experimental.pallas import tpu as pltpu
from jax.sharding import PartitionSpec as P

MODES = 256
NPTS = 32768
COUPLING = 0.8
ABSORB_RATE = 0.3
WAVE_SCALE = 0.8

G = 8
D = 16
C = 8
LZ = 96
R = 8
K = 512
NY = 128
KEEP = 3

bf16 = jnp.bfloat16
f32 = jnp.float32
VMEM = pltpu.VMEM


def whole(space=VMEM):
    return pl.BlockSpec(memory_space=space)


def params(mib):
    return pltpu.CompilerParams(vmem_limit_bytes=mib * 2**20)


def dot_t(x, h):
    return lax.dot_general(x, h, (((1,), (1,)), ((), ())), preferred_element_type=f32)


def prepare_kernel(rhs_ref, profile_ref, x_ref, chunk_ref):
    for a in range(2):
        for x in range(2):
            cols = pl.ds(a * 256 + x * NY, NY)
            for r in range(R):
                x_ref[pl.ds(r * LZ, LZ), cols] = rhs_ref[a, r, pl.ds(x, LZ, stride=2), :].astype(bf16)
    head = jnp.concatenate([rhs_ref[a, :, x, :] for a in range(2) for x in range(2)], axis=1)
    profile = profile_ref[...].astype(f32)
    gap = jnp.zeros((8, NY - LZ), f32)
    tail = jnp.concatenate([profile[:8], gap, profile[8:], gap, jnp.zeros((8, K - 2 * NY), f32)], axis=1)
    chunk = jnp.concatenate([head, tail], axis=0).astype(bf16)
    for i in range(D):
        chunk_ref[i] = chunk


def prepare(rhs, profile):
    return pl.pallas_call(
        prepare_kernel,
        out_shape=(jax.ShapeDtypeStruct((R * LZ, K), bf16), jax.ShapeDtypeStruct((D, 16, K), bf16)),
        in_specs=[whole(), whole()],
        out_specs=(whole(), whole()),
        compiler_params=params(8),
    )(rhs, profile)


def arrange_kernel(blocks_ref, h_ref, in_buf, out_buf, in_sem, out_sem):
    m = lax.broadcasted_iota(jnp.int32, (256, 256), 0)
    n = lax.broadcasted_iota(jnp.int32, (256, 256), 1)
    swap = ((m // 16 == n % 16) & (m % 16 == n // 16)).astype(f32).astype(bf16)

    def rows(i):
        return pl.ds(pl.multiple_of(i * 32, 32), 32)

    def load(i):
        return pltpu.make_async_copy(blocks_ref.at[rows(i)], in_buf.at[i], in_sem.at[i])

    def store(i):
        return pltpu.make_async_copy(out_buf.at[:, :, rows(i)], h_ref.at[:, :, rows(i)], out_sem.at[i])

    for i in range(K // 32):
        load(i).start()

    @pl.loop(0, K // 32)
    def _(i):
        load(i).wait()
        for s in range(2):
            for half in range(2):
                tile = jnp.concatenate(
                    [in_buf[i, pl.ds(s * 16, 16), c, pl.ds(half * 16, 16), :].reshape(256, NY) for c in range(2)], axis=1
                )
                moved = jnp.dot(swap, tile, preferred_element_type=f32).astype(bf16)
                for q in range(16):
                    p = half * 16 + q
                    source = p // 2
                    into = pl.ds(pl.multiple_of(i * 32 + s * 16, 16), 16)
                    for c in range(2):
                        out_buf[source % 2, source // 2, into, pl.ds(c * 256 + (p % 2) * NY, NY)] = moved[
                            q * 16 : (q + 1) * 16, c * NY : (c + 1) * NY
                        ]
        store(i).start()

    for i in range(K // 32):
        store(i).wait()


def arrange(blocks):
    return pl.pallas_call(
        arrange_kernel,
        out_shape=jax.ShapeDtypeStruct((2, C, K, K), bf16),
        in_specs=[whole(pltpu.HBM)],
        out_specs=whole(pltpu.HBM),
        scratch_shapes=[
            VMEM((K // 32, 32, 2, 32, NY), bf16),
            VMEM((2, C, K, K), bf16),
            pltpu.SemaphoreType.DMA((K // 32,)),
            pltpu.SemaphoreType.DMA((K // 32,)),
        ],
        compiler_params=params(50),
        cost_estimate=pl.CostEstimate(flops=4 * 10**9, bytes_accessed=17 * 10**6, transcendentals=0),
    )(blocks)


COST = pl.CostEstimate(flops=10**8, bytes_accessed=5 * 10**6, transcendentals=0)


def fetch(h_ref, buf, sem, core, first=0):
    copies = [pltpu.make_async_copy(h_ref.at[core, k], buf.at[k], sem.at[k]) for k in range(first, C)]
    for copy in copies:
        copy.start()
    return copies


def first_kernel(core_ref, h_ref, x_ref, v_ref, out_ref, keep_ref, even, odd, even_sem, odd_sem):
    bufs = (even, odd)
    copies = [fetch(h_ref, bufs[core], (even_sem, odd_sem)[core], core) for core in range(2)]
    acc = jnp.zeros((16, K), f32)
    for core in range(2):
        for k in range(C):
            copies[core][k].wait()
            acc = acc + dot_t(x_ref[2 * k + core], bufs[core][k])
    v = acc[:R]
    v_ref[...] = v
    for i in range(D):
        out_ref[i] = v.astype(bf16)
    for core in range(2):

        @pl.when(core_ref[0] == core)
        def _():
            for k in range(KEEP):
                keep_ref[k] = bufs[core][k]


HALF = [VMEM((C, K, K), bf16)]
SEMS = [pltpu.SemaphoreType.DMA((C,))]


def first_product(core, h, x):
    return pl.pallas_call(
        first_kernel,
        out_shape=MATVEC_OUT + (jax.ShapeDtypeStruct((KEEP, K, K), bf16),),
        in_specs=[whole(pltpu.SMEM), whole(pltpu.HBM), whole()],
        out_specs=(whole(),) * 3,
        scratch_shapes=HALF * 2 + SEMS * 2,
        compiler_params=params(50),
        cost_estimate=COST,
    )(core, h, x)


def own_kernel(core_ref, h_ref, keep_ref, x_ref, acc_ref, buf, sem):
    copies = fetch(h_ref, buf, sem, core_ref[0], KEEP)
    acc = jnp.zeros((R, K), f32)
    for k in range(KEEP):
        acc = acc + dot_t(x_ref[k], keep_ref[k])
    for k in range(KEEP, C):
        copies[k - KEEP].wait()
        acc = acc + dot_t(x_ref[k], buf[k])
    acc_ref[...] = acc


def own_half(core, h, keep, x):
    return pl.pallas_call(
        own_kernel,
        out_shape=jax.ShapeDtypeStruct((R, K), f32),
        in_specs=[whole(pltpu.SMEM), whole(pltpu.HBM), whole(), whole()],
        out_specs=whole(),
        scratch_shapes=HALF + SEMS,
        compiler_params=params(50),
        cost_estimate=COST,
    )(core, h, keep, x)


def other_kernel(core_ref, mine_ref, h_ref, x_ref, half_ref, base_ref, old_ref, v_ref, out_ref, buf, sem, ends_ref=None):
    acc = half_ref[...]
    for k, copy in enumerate(fetch(h_ref, buf, sem, 1 - core_ref[0])):
        copy.wait()
        acc = acc + dot_t(x_ref[k], buf[k])
    v = jnp.where(mine_ref[0] > 0, base_ref[...] + COUPLING * acc, old_ref[...])
    v_ref[...] = v
    rounded = v.astype(bf16)
    if ends_ref is None:
        for i in range(D):
            out_ref[i] = rounded
        return
    out_ref[...] = rounded
    low = jnp.concatenate([rounded[:, :NY], rounded[:, 2 * NY : 3 * NY]], axis=1)
    high = jnp.concatenate([rounded[:, NY : 2 * NY], rounded[:, 3 * NY :]], axis=1)
    odd = core_ref[0] > 0
    ends_ref[0] = jnp.where(odd, high, low)
    ends_ref[1] = jnp.where(odd, low, high)


def final_kernel(core_ref, mine_ref, h_ref, x_ref, half_ref, base_ref, old_ref, v_ref, out_ref, ends_ref, buf, sem):
    other_kernel(core_ref, mine_ref, h_ref, x_ref, half_ref, base_ref, old_ref, v_ref, out_ref, buf, sem, ends_ref)


MATVEC_OUT = (jax.ShapeDtypeStruct((R, K), f32), jax.ShapeDtypeStruct((D, R, K), bf16))


def other_half(core, mine, h, x, half, base, old, final):
    out = MATVEC_OUT
    if final:
        out = (out[0], jax.ShapeDtypeStruct((R, K), bf16), jax.ShapeDtypeStruct((2, R, 256), bf16))
    return pl.pallas_call(
        final_kernel if final else other_kernel,
        out_shape=out,
        in_specs=[whole(pltpu.SMEM)] * 2 + [whole(pltpu.HBM)] + [whole()] * 4,
        out_specs=(whole(),) * len(out),
        scratch_shapes=HALF + SEMS,
        compiler_params=params(50),
        cost_estimate=COST,
    )(core, mine, h, x, half, base, old)


def fronts_kernel(
    core_ref, x_ref, h_ref, behind_ref, y_out, inner_out, outer_out, last_ref, y_ref, inner_ref, outer_ref, x_buf, h_buf, x_sem, h_sem, out_sem
):
    def loads(i):
        core, chip = lax.rem(lax.div(i, 2), 2), lax.div(i, 4) * 2 + lax.rem(i, 2)
        return (
            pltpu.make_async_copy(x_ref.at[i], x_buf.at[i], x_sem.at[i]),
            pltpu.make_async_copy(h_ref.at[core, chip], h_buf.at[i], h_sem.at[i]),
        )

    @pl.loop(0, D)
    def _(i):
        for copy in loads(i):
            copy.start()

    y_ref[...] = jnp.zeros((R, LZ, K), f32)

    @pl.loop(0, D // 2)
    def _(j):
        for i in (2 * j, 2 * j + 1):
            for copy in loads(i):
                copy.wait()
        total = dot_t(x_buf[2 * j], h_buf[2 * j]) + dot_t(x_buf[2 * j + 1], h_buf[2 * j + 1])
        y_ref[...] += total.reshape(R, LZ, K)

    stores = [
        pltpu.make_async_copy(y_ref, y_out, out_sem.at[0]),
        pltpu.make_async_copy(inner_ref, inner_out, out_sem.at[1]),
        pltpu.make_async_copy(outer_ref, outer_out, out_sem.at[2]),
    ]
    stores[0].start()
    odd = core_ref[0] > 0
    for r in range(R):
        for a in range(2):
            low = y_ref[r, :, a * 256 : a * 256 + NY].astype(bf16)
            high = y_ref[r, :, a * 256 + NY : a * 256 + 256].astype(bf16)
            inner_ref[r, a] = jnp.where(odd, low, high)
            outer_ref[r, a] = jnp.where(odd, high, low)
    for store in stores[1:]:
        store.start()
    last_ref[...] = jnp.concatenate([y_ref[r, LZ - 1 : LZ, :] for r in range(R)], axis=0).astype(bf16)
    for store in stores:
        store.wait()


def fronts_of(core, x, h, behind):
    halo = jax.ShapeDtypeStruct((R, 2, LZ, NY), bf16)
    return pl.pallas_call(
        fronts_kernel,
        out_shape=(jax.ShapeDtypeStruct((R, LZ, K), f32), halo, halo, jax.ShapeDtypeStruct((R, K), bf16)),
        in_specs=[whole(pltpu.SMEM), whole(pltpu.HBM), whole(pltpu.HBM), whole(pl.ANY)],
        out_specs=(whole(pltpu.HBM),) * 3 + (whole(),),
        scratch_shapes=[
            VMEM((R, LZ, K), f32),
            VMEM((R, 2, LZ, NY), bf16),
            VMEM((R, 2, LZ, NY), bf16),
            VMEM((D, R * LZ, K), bf16),
            VMEM((D, K, K), bf16),
            pltpu.SemaphoreType.DMA((D,)),
            pltpu.SemaphoreType.DMA((D,)),
            pltpu.SemaphoreType.DMA((3,)),
        ],
        compiler_params=params(52),
        cost_estimate=pl.CostEstimate(flops=6 * 10**9, bytes_accessed=23 * 10**6, transcendentals=0),
    )(core, x, h, behind)


def wave_kernel(x_ref, coef_ref, panel_ref, behind_ref, out_ref):
    chunks = [x_ref[i].astype(f32)[8:] for i in range(D)]
    profile = jnp.concatenate([x[:, k * NY : k * NY + LZ] for x in chunks for k in range(2)], axis=0)
    panel = panel_ref[...]
    for r in range(R):
        weights = profile * coef_ref[:, r : r + 1]
        log = jnp.zeros((LZ, 256), f32)
        for _ in range(3):
            term = weights.astype(bf16)
            weights = weights - term.astype(f32)
            log = log + lax.dot_general(term, panel, (((0,), (0,)), ((), ())), preferred_element_type=f32)
        out_ref[r] = WAVE_SCALE * jnp.exp(-2.0 * log)


def wave(x, coef, panel, behind):
    return pl.pallas_call(
        wave_kernel,
        out_shape=jax.ShapeDtypeStruct((R, LZ, 256), f32),
        in_specs=[whole()] * 3 + [whole(pl.ANY)],
        out_specs=whole(),
        compiler_params=params(8),
        cost_estimate=pl.CostEstimate(flops=3 * 10**8, bytes_accessed=2 * 10**6, transcendentals=2 * 10**5),
    )(x, coef, panel, behind)


def residual_kernel(core_ref, y_ref, rhs_ref, inner_ref, outer_ref, prev_ref, v_ref, nl_ref, vi_ref, vo_ref, wave_ref, sol_ref, res_ref):
    odd = core_ref[0] > 0
    row = lax.broadcasted_iota(jnp.int32, (LZ, NY), 0)
    lane = lax.broadcasted_iota(jnp.int32, (LZ, NY), 1)
    for r in range(R):
        s = {}
        for a in range(2):
            for x in range(2):
                cols = slice(a * 256 + x * NY, a * 256 + (x + 1) * NY)
                s[a, x] = jnp.where(row == 0, v_ref[r : r + 1, cols], y_ref[r, :, cols])
        lap = {}
        for a in range(2):
            ends = slice(a * NY, (a + 1) * NY)
            inner = jnp.where(row == 0, vi_ref[r : r + 1, ends].astype(f32), inner_ref[r, a].astype(f32))
            outer = jnp.where(row == 0, vo_ref[r : r + 1, ends].astype(f32), outer_ref[r, a].astype(f32))
            below, above = jnp.where(odd, inner, outer), jnp.where(odd, outer, inner)
            for x in range(2):
                cols = slice(a * 256 + x * NY, a * 256 + (x + 1) * NY)
                own = s[a, x]
                before = jnp.where(row == 0, prev_ref[r : r + 1, cols].astype(f32), pltpu.roll(own, 1, 0))
                after = jnp.where(row == LZ - 1, nl_ref[r : r + 1, cols].astype(f32), pltpu.roll(own, LZ - 1, 0))
                left = jnp.where(lane == 0, 0.0, pltpu.roll(own, 1, 1))
                right = jnp.where(lane == NY - 1, 0.0, pltpu.roll(own, NY - 1, 1))
                beside = before + after + left + right
                beside = beside + (below if x == 0 else s[a, 0]) + (s[a, 1] if x == 0 else above)
                lap[a, x] = 6.0 * own - beside
        for x in range(2):
            w = wave_ref[r, :, x * NY : (x + 1) * NY]
            rows = pl.ds(x, LZ, stride=2)
            real = lap[0, x] - w * s[0, x] + ABSORB_RATE * w * s[1, x]
            imag = lap[1, x] - w * s[1, x] - ABSORB_RATE * w * s[0, x]
            sol_ref[0, r, rows, :] = s[0, x]
            sol_ref[1, r, rows, :] = s[1, x]
            res_ref[0, r, rows, :] = rhs_ref[0, r, rows, :] - real
            res_ref[1, r, rows, :] = rhs_ref[1, r, rows, :] - imag


def residual(*args):
    shape = jax.ShapeDtypeStruct((2, R, 2 * LZ, NY), f32)
    return pl.pallas_call(
        residual_kernel,
        out_shape=(shape, shape),
        in_specs=[whole(pltpu.SMEM)] + [whole()] * (len(args) - 1),
        out_specs=(whole(), whole()),
        compiler_params=params(24),
    )(*args)


def pair_groups(step):
    groups = []
    for k in range(G // 2):
        first = (2 * k + step - 1) % G
        second = (first + 1) % G
        for core in range(2):
            groups.append([g * D + 2 * i + core for g in (first, second) for i in range(C)])
    return groups


def shift(value, axis, by):
    size = lax.axis_size(axis)
    return lax.ppermute(value, axis, [(i, i + by) for i in range(size) if 0 <= i + by < size])


def shards(rhs, inverse_blocks, mode_panel, mode_profile, generator, lattice_index, shift_index):
    group = lax.axis_index("layer")
    flat = rhs.reshape(2, R, 2 * LZ, NY)
    own, chunk = prepare(flat, mode_profile)
    along_x = [[z * 4 + x * 2 + c for x in range(2)] for z in range(4) for c in range(2)]
    along_z = [[z * 4 + x * 2 + c for z in range(4) for c in range(2)] for x in range(2)]
    paired = lax.all_gather(own, "plane", axis=0, axis_index_groups=along_x)
    heads = lax.all_to_all(chunk, "plane", 0, 0)
    blocks, _ = lax.optimization_barrier((inverse_blocks, chunk))
    h = arrange(blocks.reshape(K, 2, 32, NY))
    heads, _ = lax.optimization_barrier((heads, h))

    mixed = (lattice_index[None, :] * generator[:, None] + shift_index.T) % NPTS
    amplitude = 0.25 / jnp.sqrt(1.0 + jnp.arange(MODES, dtype=f32) / 8.0)
    coef = amplitude[:, None] * ((mixed.astype(f32) + 0.5) / NPTS - 0.5)
    core = lax.rem(lax.axis_index("plane"), 2).astype(jnp.int32).reshape(1)
    twin = [(i, i ^ 1) for i in range(D)]
    next_chip = [(i, i + 1) for i in range(1, D - 1, 2)] + [(i + 1, i) for i in range(1, D - 1, 2)]

    base, out, keep = first_product(core, h, heads)
    v = base
    for step in range(1, G):
        if step == 2:
            paired, _ = lax.optimization_barrier((paired, v))
            gathered = lax.all_gather(paired, "plane", axis=0, axis_index_groups=along_z).reshape(D, R * LZ, K)
        got = lax.all_to_all(out, ("layer", "plane"), 0, 0, axis_index_groups=pair_groups(step))
        if step == 2:
            wavenum = wave(heads, coef, mode_panel.reshape(MODES, 256), v)
            got, wavenum = lax.optimization_barrier((got, wavenum))
        if step == 6:
            y, inner, outer, last = fronts_of(core, gathered, h, v)
            got, inner, outer, last = lax.optimization_barrier((got, inner, outer, last))
        if step == 7:
            last, v = lax.optimization_barrier((last, v))
            last = shift(last, "layer", 1)
            got, inner, outer, last = lax.optimization_barrier((got, inner, outer, last))
            outer = lax.ppermute(outer, "plane", next_chip)
            inner = lax.ppermute(inner, "plane", twin)
        other = lax.ppermute(got, "plane", twin)
        half = own_half(core, h, keep, got)
        mine = (group == step).astype(jnp.int32).reshape(1)
        v, out, *ends = other_half(core, mine, h, other, half, base, v, step == G - 1)

    v_outer = lax.ppermute(ends[0][0], "plane", next_chip)
    v_next = shift(out, "layer", -1)
    v_inner = lax.ppermute(ends[0][1], "plane", twin)
    sol, res = residual(core, y, flat, inner, outer, last, v, v_next, v_inner, v_outer, wavenum)
    return sol.reshape(rhs.shape), res.reshape(rhs.shape)


def solution(mesh):
    return jax.shard_map(
        shards,
        mesh=mesh,
        in_specs=(
            P(None, None, "layer", "plane", None),
            P("layer", None, "plane", None, None, None, None),
            P(None, "plane", None),
            P("plane", "layer"),
            P(),
            P(),
            P(),
        ),
        out_specs=(P(None, None, "layer", "plane", None), P(None, None, "layer", "plane", None)),
        check_vma=False,
    )
```
